128 devices in a mesh: seq: 16 (over y_hi, x, core), tp: 8 (over y_lo, z).
Axes of the slice: x: 4, y: 4 (y_hi: 2, y_lo: 2; y = y_hi * 2 + y_lo), z: 4, core: 2. Of those that a mesh axis runs over, the one named last changes fastest.
Arguments:
- hidden: bfloat16 [8192, 2560], P('seq', 'tp'), may hold values from -6 to 6
- norm_gain: float32 [2560], replicated, may hold values from 0.25 to 1.75
- query_weight: float32 [2560, 4096], P('seq', 'tp'), may hold values from -0.125 to 0.125
- key_weight: float32 [2560, 1024], P('seq', 'tp'), may hold values from -0.125 to 0.125
- value_weight: float32 [2560, 1024], P('seq', 'tp'), may hold values from -0.125 to 0.125
- query_gain: float32 [128], replicated, may hold values from 0.5 to 8
- key_gain: float32 [128], replicated, may hold values from 0.5 to 8
- lengths: int32 [8], replicated, may hold values from 1 to 4096, 8192 in all
- page_table: int32 [64], replicated, may hold values from 0 to 63, each once
Outputs:
- attention: bfloat16 [8192, 4096], P('seq', 'tp')
- key_cache: bfloat16 [64, 8, 128, 128], P('seq', 'tp')
- value_cache: bfloat16 [64, 8, 128, 128], P('seq', 'tp')
The draws below stay inside these ranges and needn't reach their ends.
Inputs may be any that keep to these rules, and one draw needn't show every extreme that they name: 8 positive lengths summing to 8192; the longest is exactly 4096. `page_table`: every page is named by exactly one block.
All inputs are finite; a program needn't handle non-finite values.
Results may differ from the reference program's by a relative error of at most 0.0085.
The reference program's roundings to bfloat16 on the way count: a program that leaves them out, or rounds other values in their place, can miss the bound.
Values may be sent and summed in bfloat16 or wider, within the bound.
A program may use at most 128 MiB of HBM per device.

```python
import math
import jax
import jax.numpy as jnp
import numpy as np
from jax import lax

D = 2560
QH = 32
KVH = 8
HD = 128
PAGE = 128
NSEG = 8
TOKENS = 8192
PAGES = 64
MOST = 4096


def gain_values(key):
    return jnp.exp(jax.random.uniform(key, (HD,), jnp.float32, math.log(0.5), math.log(2.0)))


def draw_query_gain(key, part):
    return gain_values(jax.random.fold_in(key, 11))


def draw_key_gain(key, part):
    return gain_values(jax.random.fold_in(key, 23))


def block_scale(rng, extent, pieces, smallest, top_value):
    level = 1.0
    for dim, blocks in pieces:
        heights = jax.random.uniform(jax.random.fold_in(jax.random.fold_in(rng, 6), dim), (blocks,), jnp.float32, smallest / len(pieces), top_value / len(pieces))
        level = level * jnp.repeat(jnp.exp(heights), extent[dim] // blocks).reshape((-1,) + (1,) * (len(extent) - 1 - dim))
    return level


def split_up(amount, total, most, slope):
    loads = [(1 << 20) // math.isqrt(standing ** slope) + 1 for standing in range(2, amount + 1)]
    surplus, counts = total - most - (amount - 1), [1] * (amount - 1)
    while surplus > 0:
        free = [i for i in range(amount - 1) if counts[i] < most]
        pool, left = sum([loads[i] for i in free]), surplus
        for i in free:
            extra = min(most - counts[i], max(1, left * loads[i] // pool), surplus)
            counts[i] = counts[i] + extra
            surplus = surplus - extra
    return np.array([most] + counts)


def ragged(own_key, number_of, total, most, slope):
    if number_of == 2:
        one = jax.random.randint(own_key, (), max(1, total - most), min(most, total - 1) + 1)
        return jnp.stack([one, total - one])
    sizes = jnp.asarray(split_up(number_of, total, most, slope), jnp.int32)
    pairs = (number_of - 1) // 2
    donor, taker = sizes[1:1 + 2 * pairs:2], sizes[2:2 + 2 * pairs:2]
    margin = jnp.minimum(donor - 1, most - taker)
    passed = jax.random.randint(jax.random.fold_in(own_key, 1), (pairs,), 0, 1 << 20) % (margin + 1)
    sizes = sizes.at[1:1 + 2 * pairs:2].set(donor - passed).at[2:2 + 2 * pairs:2].set(taker + passed)
    return sizes[jax.random.permutation(jax.random.fold_in(own_key, 2), number_of)]


def bell_draw(key, shape, scale, limit, cuts=(), kind=jnp.bfloat16):
    loudness = block_scale(key, shape, cuts, -0.22, 0.18) if cuts else 1.0
    drawn = jax.random.normal(key, shape, jnp.float32) * scale * loudness
    return jnp.minimum(jnp.maximum(drawn, -limit), limit).astype(kind)


def setup_inputs(seed: int = 0) -> dict:
    keys = jax.random.split(jax.random.key(seed), 10)
    hidden = bell_draw(keys[0], (TOKENS, D), 1.0, 6.0, ((0, 16), (1, 8)))
    norm_gain = jnp.clip(1.0 + 0.15 * jax.random.normal(keys[1], (D,), jnp.float32), 0.25, 1.75)
    query_weight = bell_draw(keys[2], (D, QH * HD), D ** -0.5, 0.125, ((0, 16), (1, 8)), jnp.float32)
    key_weight = bell_draw(keys[3], (D, KVH * HD), D ** -0.5, 0.125, ((0, 16), (1, 8)), jnp.float32)
    value_weight = bell_draw(keys[4], (D, KVH * HD), D ** -0.5, 0.125, ((0, 16), (1, 8)), jnp.float32)
    query_gain = draw_query_gain(jax.random.fold_in(keys[9], 71), 0)
    key_gain = draw_key_gain(jax.random.fold_in(keys[9], 71), 0)
    lengths = ragged(keys[7], NSEG, TOKENS, MOST, 2).astype(jnp.int32)
    page_table = jax.random.permutation(keys[8], PAGES).astype(jnp.int32)
    return {"hidden": hidden, "norm_gain": norm_gain, "query_weight": query_weight, "key_weight": key_weight, "value_weight": value_weight, "query_gain": query_gain, "key_gain": key_gain, "lengths": lengths, "page_table": page_table}


epsilon = 1e-06
excluded = -1e+30

def segment_of(slot_index, prompt_ends):
    return lax.optimization_barrier(jnp.sum((slot_index[..., None] >= prompt_ends).astype(jnp.int32), axis=-1))

def position_of(slot_index, prompt_ends, lengths):
    segment_id = segment_of(slot_index, prompt_ends)
    prompt_starts = prompt_ends - lengths
    labels = jnp.arange(lengths.shape[0], dtype=jnp.int32)
    picked = lax.optimization_barrier(jnp.sum(jnp.where(segment_id[..., None] == labels, prompt_starts, 0), axis=-1))
    return (segment_id, slot_index - picked)

def head_norm(vectors, gain):
    mean_sq = lax.optimization_barrier(jnp.mean(vectors * vectors, axis=-1, keepdims=True))
    return vectors * lax.rsqrt(mean_sq + epsilon) * gain

def rotate(vectors, position):
    head_dim = vectors.shape[-1]
    half_dim = head_dim // 2
    frequency = 1000000.0 ** (-(jnp.arange(half_dim, dtype=jnp.float32) * 2.0 / head_dim))
    angles = position.astype(jnp.float32)[:, None] * frequency[None, :]
    cosine = jnp.cos(angles)[:, None, :]
    sine_part = jnp.sin(angles)[:, None, :]
    front = vectors[..., :half_dim]
    back_half = vectors[..., half_dim:]
    return jnp.concatenate([front * cosine - back_half * sine_part, back_half * cosine + front * sine_part], axis=-1)

def reference(hidden, norm_gain, query_weight, key_weight, value_weight, query_gain, key_gain, lengths, page_table):
    widened = hidden.astype(jnp.float32)
    normed = (widened * lax.rsqrt(lax.optimization_barrier(jnp.mean(widened * widened, axis=-1, keepdims=True)) + epsilon) * norm_gain).astype(jnp.bfloat16)
    server_block = jnp.concatenate([query_weight, key_weight, value_weight], axis=1).astype(jnp.bfloat16)
    projected = jnp.dot(normed, server_block, preferred_element_type=jnp.float32)
    query_cols = QH * HD
    key_cols = KVH * HD
    slot_index = jnp.arange(TOKENS, dtype=jnp.int32)
    prompt_ends = jnp.cumsum(lengths).astype(jnp.int32)
    segment_id, position = position_of(slot_index, prompt_ends, lengths)
    queries = rotate(head_norm(projected[:, :query_cols].reshape(TOKENS, QH, HD), query_gain), position).astype(jnp.bfloat16)
    key_rows = rotate(head_norm(projected[:, query_cols:query_cols + key_cols].reshape(TOKENS, KVH, HD), key_gain), position).astype(jnp.bfloat16)
    values = projected[:, query_cols + key_cols:].reshape(TOKENS, KVH, HD).astype(jnp.bfloat16)
    group_size = QH // KVH
    row_block = math.gcd(TOKENS, 2048)
    block_count = TOKENS // row_block

    def one_block(index):
        head = index // block_count
        first = index % block_count * row_block
        query_block = lax.dynamic_slice_in_dim(queries[:, head, :], first, row_block, 0)
        row_slots = lax.dynamic_slice_in_dim(slot_index, first, row_block, 0)
        row_segments = lax.dynamic_slice_in_dim(segment_id, first, row_block, 0)
        key_block = key_rows[:, head // group_size, :]
        value_block = values[:, head // group_size, :]
        allowed = (segment_id[None, :] == row_segments[:, None]) & (slot_index[None, :] <= row_slots[:, None])
        scores = jnp.dot(query_block, key_block.T, preferred_element_type=jnp.float32) * HD ** (-0.5)
        running_max = lax.optimization_barrier(jnp.max(jnp.where(allowed, scores, excluded), axis=1, keepdims=True))
        weights = jnp.where(allowed, jnp.exp(scores - running_max), 0.0)
        summed = jnp.dot(weights.astype(jnp.bfloat16), value_block, preferred_element_type=jnp.float32)
        return summed / lax.optimization_barrier(jnp.sum(weights, axis=1, keepdims=True))
    blocks = lax.map(one_block, jnp.arange(QH * block_count, dtype=jnp.int32))
    heads = blocks.reshape(QH, TOKENS, HD)
    attention = heads.transpose(1, 0, 2).reshape(TOKENS, query_cols).astype(jnp.bfloat16)
    key_blocks = key_rows.reshape(PAGES, PAGE, KVH, HD).transpose(0, 2, 1, 3)
    value_blocks = values.reshape(PAGES, PAGE, KVH, HD).transpose(0, 2, 1, 3)
    key_cache = jnp.zeros_like(key_blocks).at[page_table].set(key_blocks)
    value_cache = jnp.zeros_like(value_blocks).at[page_table].set(value_blocks)
    return (attention, key_cache, value_cache)
```

```python
import math

import jax
import jax.numpy as jnp
import numpy as np
from jax import lax
from jax.experimental import pallas as pl
from jax.experimental.pallas import tpu as pltpu
from jax.sharding import PartitionSpec as P

T = 512
F = 320
D = 2560
WR = 160
HD = 128
G = 4
NC = 768
PAGE = 128
PAGES = 64
NSEG = 8
SEQ = 16
TP = 8
EPS = 1e-6
EXCLUDED = -1e30
HR = 640
MESH = pl.DeviceIdType.MESH
SCALE = HD**-0.5 * math.log2(math.e)
VE = HD + 16


def kernel(
    hid_ref,
    gain_ref,
    wq_ref,
    wk_ref,
    wv_ref,
    qg_ref,
    kg_ref,
    freq_ref,
    len_ref,
    pt_ref,
    out_ref,
    kc_ref,
    vc_ref,
    hall,
    wall,
    kv,
    hn,
    qt,
    acc,
    mx,
    cosr,
    sinr,
    startr,
    ssq,
    h_send,
    h_recv,
    w_send,
    w_recv,
    kv_send,
    kv_recv,
):
    s = lax.axis_index("seq")
    t = lax.axis_index("tp")
    yh, x, c = s // 8, (s // 2) % 4, s % 2
    yl, z = t // 4, t % 4

    def seq_rank(dx, dy, dc):
        return ((yh + dy) % 2) * 8 + ((x + dx) % 4) * 2 + (c + dc) % 2

    def tp_rank(dz, dy):
        return ((yl + dy) % 2) * 4 + (z + dz) % 4

    sib = {"seq": seq_rank(0, 0, 1), "tp": t}
    xp = {"seq": seq_rank(1, 0, 0), "tp": t}
    xm = {"seq": seq_rank(3, 0, 0), "tp": t}
    yhp = {"seq": seq_rank(0, 1, 0), "tp": t}
    zp = {"seq": s, "tp": tp_rank(1, 0)}
    zm = {"seq": s, "tp": tp_rank(3, 0)}
    ylp = {"seq": s, "tp": tp_rank(0, 1)}
    barrier = pltpu.get_barrier_semaphore()
    for peer in (sib, xp, xm, yhp, zp, zm, ylp):
        pl.semaphore_signal(barrier, inc=1, device_id=peer, device_id_type=MESH)

    hall[t, 0:T, :] = hid_ref[:, 0:256]
    for q in range(4):
        hall[t, T : T + 128, 64 * q : 64 * q + 64] = hid_ref[128 * q : 128 * q + 128, 256:320]
    own_w = pl.ds(pl.multiple_of(s * WR, 16), WR)
    wall[own_w, 0:512] = wq_ref[...].astype(jnp.bfloat16)
    wall[own_w, 512:640] = wk_ref[...].astype(jnp.bfloat16)
    wall[own_w, 640:768] = wv_ref[...].astype(jnp.bfloat16)

    pl.semaphore_wait(barrier, 7)

    started = []

    class Gather:
        def __init__(self, region, send, recv):
            self.region, self.send, self.recv, self.sends = region, send, recv, 0

        def go(self, rank, half, role, peer):
            ref = self.region(rank, half)
            copy = pltpu.make_async_remote_copy(
                src_ref=ref,
                dst_ref=ref,
                send_sem=self.send.at[self.sends],
                recv_sem=self.recv.at[role],
                device_id=peer,
                device_id_type=MESH,
            )
            self.sends += 1
            copy.start()
            started.append(copy)

        def wait(self, rank, half, role):
            ref = self.region(rank, half)
            pltpu.make_async_remote_copy(
                src_ref=ref,
                dst_ref=ref,
                send_sem=self.send.at[0],
                recv_sem=self.recv.at[role],
                device_id=sib,
                device_id_type=MESH,
            ).wait_recv()

    def h_region(rank, half):
        if half is None:
            return hall.at[rank]
        return hall.at[rank, pl.ds(half * (HR // 2), HR // 2), :]

    def w_region(rank, half):
        if half is None:
            return wall.at[pl.ds(pl.multiple_of(rank * WR, 16), WR), :]
        return wall.at[pl.ds(pl.multiple_of(rank * WR + half * (WR // 2), 16), WR // 2), :]

    def kv_region(rank, half):
        if half is None:
            return kv.at[pl.ds(rank * 8, 8)]
        return kv.at[pl.ds(rank * 8 + half * 4, 4)]

    seq_roles = [(0, 1, None), (3, 0, None), (3, 1, None), (1, 0, None), (1, 1, None), (2, 0, 0), (2, 1, 0), (2, 0, 1), (2, 1, 1)]
    seq_forward = {
        0: ((None, 2, xp), (None, 4, xm)),
        1: ((0, 5, xp),),
        2: ((0, 6, xp),),
        3: ((1, 7, xm),),
        4: ((1, 8, xm),),
    }

    def seq_begin(g):
        rank = seq_rank(0, 0, 0)
        g.go(rank, None, 0, yhp)
        g.go(rank, None, 1, xp)
        g.go(rank, None, 3, xm)
        g.go(rank, None, 10, sib)

    def seq_pass(g, role):
        dx, dy, half = seq_roles[role]
        rank = seq_rank(dx, dy, 0)
        g.wait(rank, half, role)
        for part, to, peer in seq_forward.get(role, ()):
            g.go(rank, part, to, peer)
        g.go(rank, half, 11 + role, sib)

    def seq_sib(g, role):
        if role is None:
            g.wait(seq_rank(0, 0, 1), None, 10)
        else:
            dx, dy, half = seq_roles[role]
            g.wait(seq_rank(dx, dy, 1), half, 11 + role)

    tp_roles = [(0, 1, None), (3, 0, None), (3, 1, None), (1, 0, None), (1, 1, None), (2, 0, 0), (2, 0, 1), (2, 1, 0), (2, 1, 1)]
    tp_forward = {
        0: ((None, 2, zp), (None, 4, zm)),
        1: ((0, 5, zp),),
        3: ((1, 6, zm),),
        5: ((0, 7, ylp),),
        6: ((1, 8, ylp),),
    }

    def tp_pass(g, role):
        dz, dy, half = tp_roles[role]
        rank = tp_rank(dz, dy)
        g.wait(rank, half, role)
        for part, to, peer in tp_forward.get(role, ()):
            g.go(rank, part, to, peer)

    gh = Gather(h_region, h_send, h_recv)
    gw = Gather(w_region, w_send, w_recv)
    gk = Gather(kv_region, kv_send, kv_recv)

    gh.go(t, None, 0, ylp)
    gh.go(t, None, 1, zp)
    gh.go(t, None, 3, zm)
    seq_begin(gw)

    def start_of(slots):
        start = jnp.zeros_like(slots)
        end = jnp.int32(0)
        for i in range(NSEG):
            end = end + len_ref[i]
            start = jnp.where(slots >= end, end, start)
        return start

    rows = s * T + lax.broadcasted_iota(jnp.int32, (T, HD), 0)
    position = (rows - start_of(rows)).astype(jnp.float32)
    angles = position * freq_ref[...]
    cosr[...] = jnp.cos(angles)
    lane = lax.broadcasted_iota(jnp.int32, (T, HD), 1)
    sine = jnp.sin(angles)
    sinr[...] = jnp.where(lane < HD // 2, -sine, sine)
    slots = s * T + lax.broadcasted_iota(jnp.int32, (8, T), 1)
    startr[...] = start_of(slots)

    per = T // PAGE
    source = [jnp.int32(0)] * per
    for b in range(PAGES):
        page = pt_ref[b] - s * per
        row = (b // per) * 2 * per + b % per
        source = [jnp.where(page == i, row, f) for i, f in enumerate(source)]

    ssq[...] = jnp.zeros_like(ssq)

    def add_squares(rank):
        v = hall[rank, 0:T, :].astype(jnp.float32)
        v = v * v
        ssq[...] += v[:, 0:HD] + v[:, HD:]

    add_squares(t)
    tp_pass(gh, 0)
    seq_pass(gw, 0)
    tp_pass(gh, 1)
    tp_pass(gh, 3)
    seq_pass(gw, 1)
    seq_pass(gw, 3)
    seq_sib(gw, None)
    tp_pass(gh, 5)
    tp_pass(gh, 6)
    seq_pass(gw, 2)
    seq_pass(gw, 4)
    for dz, dy in ((0, 1), (1, 0), (3, 0), (2, 0)):
        add_squares(tp_rank(dz, dy))
    for role in (5, 7, 6, 8):
        seq_pass(gw, role)
    for role in range(9):
        seq_sib(gw, role)
    tp_pass(gh, 2)
    add_squares(tp_rank(3, 1))
    tp_pass(gh, 4)
    add_squares(tp_rank(1, 1))
    tp_pass(gh, 7)
    tp_pass(gh, 8)
    add_squares(tp_rank(2, 1))

    half_lane = lax.broadcasted_iota(jnp.int32, (128, 128), 1) < 64
    for pair in range(TP // 2):
        for col in range(2):
            lanes = slice(128 * col, 128 * col + 128)
            a = hall[2 * pair, T : T + 128, lanes].astype(jnp.float32)
            b = hall[2 * pair + 1, T : T + 128, lanes].astype(jnp.float32)
            low = jnp.where(half_lane, a, pltpu.roll(b, 64, 1))
            high = jnp.where(half_lane, pltpu.roll(a, 64, 1), b)
            for q, v in ((2 * col, low), (2 * col + 1, high)):
                where = slice(128 * q, 128 * q + 128)
                ssq[where, :] += v * v
                hn[where, 2048 + 128 * pair : 2176 + 128 * pair] = v.astype(jnp.bfloat16)

    scale = lax.rsqrt(jnp.sum(ssq[...], axis=1, keepdims=True) * (1.0 / D) + EPS)
    for i in range(TP):
        v = hall[i, 0:T, :].astype(jnp.float32) * scale
        hn[:, 256 * i : 256 * i + 256] = (v * gain_ref[:, 256 * i : 256 * i + 256]).astype(jnp.bfloat16)
    v = hn[:, 2048:].astype(jnp.float32) * scale
    hn[:, 2048:] = (v * gain_ref[:, 2048:]).astype(jnp.bfloat16)

    def project(lo, hi):
        total = None
        for i in range(TP):
            w = wall[F * i : F * i + 256, lo:hi]
            part = jnp.dot(hn[:, 256 * i : 256 * i + 256], w, preferred_element_type=jnp.float32)
            total = part if total is None else total + part
        for i in range(2):
            w = jnp.concatenate([wall[F * j + 256 : F * j + 320, lo:hi] for j in range(4 * i, 4 * i + 4)], axis=0)
            at = 2048 + 256 * i
            total = total + jnp.dot(hn[:, at : at + 256], w, preferred_element_type=jnp.float32)
        return total

    def norm_rotate(u, gain):
        mean = jnp.sum(u * u, axis=1, keepdims=True) * (1.0 / HD)
        u = u * lax.rsqrt(mean + EPS) * gain
        return u * cosr[...] + pltpu.roll(u, HD // 2, 1) * sinr[...]

    kvp = project(512, 768)
    keys = norm_rotate(kvp[:, 0:HD], kg_ref[...]).astype(jnp.bfloat16)
    vt = kvp[:, HD:].T.astype(jnp.bfloat16)
    for i in range(T // PAGE):
        kv[s * 8 + i] = keys[PAGE * i : PAGE * i + PAGE, :]
        kv[s * 8 + per + i] = vt[:, PAGE * i : PAGE * i + PAGE]
    seq_begin(gk)

    for pair in range(G // 2):
        qp = project(256 * pair, 256 * pair + 256)
        for i in range(2):
            u = norm_rotate(qp[:, HD * i : HD * i + HD], qg_ref[...]).astype(jnp.bfloat16)
            qt[2 * pair + i] = u.astype(jnp.float32).T.astype(jnp.bfloat16)

    ones = jnp.where(lax.broadcasted_iota(jnp.int32, (VE - HD, T), 0) == 0, 1.0, 0.0).astype(jnp.bfloat16)

    def attend(rank, diagonal):
        keys = jnp.concatenate([kv[rank * 8 + i] for i in range(per)], axis=0)
        vals = jnp.concatenate([kv[rank * 8 + per + i] for i in range(per)], axis=1)
        vals = jnp.concatenate([vals, ones], axis=0)

        def head(h, carry):
            scores = jnp.dot(keys, qt[h], preferred_element_type=jnp.float32)
            key_slot = rank * T + lax.broadcasted_iota(jnp.int32, (T, T), 0)
            allowed = key_slot >= startr[0:1, :]
            if diagonal:
                query_slot = rank * T + lax.broadcasted_iota(jnp.int32, (T, T), 1)
                allowed = allowed & (key_slot <= query_slot)
            scores = jnp.where(allowed, scores, EXCLUDED)
            top = jnp.max(scores, axis=0, keepdims=True)
            if not diagonal:
                old = mx[h]
                top = jnp.maximum(old, top)
            probs = jnp.exp2((scores - top) * SCALE).astype(jnp.bfloat16)
            sums = jnp.dot(vals, probs, preferred_element_type=jnp.float32)
            if diagonal:
                acc[h] = sums
            else:
                acc[h] = acc[h] * jnp.exp2((old - top) * SCALE) + sums
            mx[h] = top
            return carry

        lax.fori_loop(0, G, head, 0)

    def attend_all(offsets):
        def one(k, carry):
            rank = seq_rank(*offsets[0])
            for i in range(1, len(offsets)):
                rank = jnp.where(k == i, seq_rank(*offsets[i]), rank)

            @pl.when((rank < s) & (rank + 8 >= s))
            def _():
                attend(rank, False)

            return carry

        lax.fori_loop(0, len(offsets), one, 0)

    attend(s, True)
    seq_pass(gk, 0)
    seq_pass(gk, 1)
    seq_pass(gk, 3)
    seq_sib(gk, None)
    attend_all([(0, 0, 1), (3, 0, 0), (1, 0, 0), (0, 1, 0)])
    seq_pass(gk, 2)
    seq_pass(gk, 4)
    for role in (0, 1, 3):
        seq_sib(gk, role)
    attend_all([(3, 0, 1), (1, 0, 1), (0, 1, 1), (3, 1, 0), (1, 1, 0)])
    for role in (5, 7, 6, 8):
        seq_pass(gk, role)
    for role in (2, 4):
        seq_sib(gk, role)
    attend_all([(3, 1, 1), (1, 1, 1), (2, 0, 0), (2, 1, 0)])
    for role in (5, 6, 7, 8):
        seq_sib(gk, role)
    attend_all([(2, 0, 1), (2, 1, 1)])

    for h in range(G):
        o = acc[h, 0:HD, :] / acc[h, HD : HD + 1, :]
        out_ref[:, HD * h : HD * h + HD] = o.T.astype(jnp.bfloat16)

    for i in range(per):
        kc_ref[i, 0] = kv[source[i]]
        page = kv[source[i] + per]
        vc_ref[i, 0] = page.astype(jnp.float32).T.astype(jnp.bfloat16)

    for copy in started:
        copy.wait_send()


def shards(hidden, norm_gain, query_weight, key_weight, value_weight, query_gain, key_gain, lengths, page_table):
    by_shard = norm_gain.reshape(TP, F)
    gain = jnp.concatenate([by_shard[:, :256].reshape(1, -1), by_shard[:, 256:].reshape(1, -1)], axis=1)
    half = 1000000.0 ** -(np.arange(HD // 2, dtype=np.float32) * np.float32(2.0 / HD))
    freq = jnp.asarray(np.concatenate([half, half])[None, :].astype(np.float32))
    vmem = pl.BlockSpec(memory_space=pltpu.VMEM)
    smem = pl.BlockSpec(memory_space=pltpu.SMEM)
    return pl.pallas_call(
        kernel,
        out_shape=(
            jax.ShapeDtypeStruct((T, G * HD), jnp.bfloat16),
            jax.ShapeDtypeStruct((T // PAGE, 1, PAGE, HD), jnp.bfloat16),
            jax.ShapeDtypeStruct((T // PAGE, 1, PAGE, HD), jnp.bfloat16),
        ),
        in_specs=[vmem] * 8 + [smem] * 2,
        out_specs=(vmem,) * 3,
        scratch_shapes=[
            pltpu.VMEM((TP, HR, 256), jnp.bfloat16),
            pltpu.VMEM((D, NC), jnp.bfloat16),
            pltpu.VMEM((SEQ * 8, PAGE, HD), jnp.bfloat16),
            pltpu.VMEM((T, D), jnp.bfloat16),
            pltpu.VMEM((G, HD, T), jnp.bfloat16),
            pltpu.VMEM((G, VE, T), jnp.float32),
            pltpu.VMEM((G, 1, T), jnp.float32),
            pltpu.VMEM((T, HD), jnp.float32),
            pltpu.VMEM((T, HD), jnp.float32),
            pltpu.VMEM((8, T), jnp.int32),
            pltpu.VMEM((T, HD), jnp.float32),
            pltpu.SemaphoreType.DMA((9,)),
            pltpu.SemaphoreType.DMA((9,)),
            pltpu.SemaphoreType.DMA((20,)),
            pltpu.SemaphoreType.DMA((20,)),
            pltpu.SemaphoreType.DMA((20,)),
            pltpu.SemaphoreType.DMA((20,)),
        ],
        compiler_params=pltpu.CompilerParams(
            collective_id=0, has_side_effects=True, vmem_limit_bytes=48 * 1024 * 1024
        ),
        cost_estimate=pl.CostEstimate(flops=7 * 10**9, bytes_accessed=4 * 10**6, transcendentals=10**7),
    )(
        hidden,
        gain,
        query_weight,
        key_weight,
        value_weight,
        query_gain.reshape(1, HD),
        key_gain.reshape(1, HD),
        freq,
        lengths,
        page_table,
    )


def solution(mesh):
    return jax.shard_map(
        shards,
        mesh=mesh,
        in_specs=(
            P("seq", "tp"),
            P(),
            P("seq", "tp"),
            P("seq", "tp"),
            P("seq", "tp"),
            P(),
            P(),
            P(),
            P(),
        ),
        out_specs=(P("seq", "tp"), P("seq", "tp", None, None), P("seq", "tp", None, None)),
        check_vma=False,
    )
```

```python
import math

import jax
import jax.numpy as jnp
import numpy as np
from jax import lax
from jax.experimental import pallas as pl
from jax.experimental.pallas import tpu as pltpu
from jax.sharding import PartitionSpec as P

T = 512
F = 320
D = 2560
WR = 160
HD = 128
G = 4
NC = 768
PAGE = 128
PAGES = 64
NSEG = 8
SEQ = 16
TP = 8
EPS = 1e-6
EXCLUDED = -1e30
HR = 640
MESH = pl.DeviceIdType.MESH
SCALE = HD**-0.5 * math.log2(math.e)
VE = HD + 16


def kernel(
    hid_ref,
    gain_ref,
    wq_ref,
    wk_ref,
    wv_ref,
    qg_ref,
    kg_ref,
    freq_ref,
    len_ref,
    pt_ref,
    out_ref,
    kc_ref,
    vc_ref,
    hall,
    wall,
    kv,
    hn,
    qt,
    acc,
    mx,
    cosr,
    sinr,
    startr,
    other,
    bounds,
    ssq,
    h_send,
    h_recv,
    w_send,
    w_recv,
    kv_send,
    kv_recv,
):
    s = lax.axis_index("seq")
    t = lax.axis_index("tp")
    yh, x, c = s // 8, (s // 2) % 4, s % 2
    yl, z = t // 4, t % 4

    def seq_rank(dx, dy, dc):
        return ((yh + dy) % 2) * 8 + ((x + dx) % 4) * 2 + (c + dc) % 2

    def tp_rank(dz, dy):
        return ((yl + dy) % 2) * 4 + (z + dz) % 4

    sib = {"seq": seq_rank(0, 0, 1), "tp": t}
    xp = {"seq": seq_rank(1, 0, 0), "tp": t}
    xm = {"seq": seq_rank(3, 0, 0), "tp": t}
    yhp = {"seq": seq_rank(0, 1, 0), "tp": t}
    zp = {"seq": s, "tp": tp_rank(1, 0)}
    zm = {"seq": s, "tp": tp_rank(3, 0)}
    ylp = {"seq": s, "tp": tp_rank(0, 1)}
    barrier = pltpu.get_barrier_semaphore()
    for peer in (sib, xp, xm, yhp, zp, zm, ylp):
        pl.semaphore_signal(barrier, inc=1, device_id=peer, device_id_type=MESH)

    hall[t, 0:T, :] = hid_ref[:, 0:256]
    for q in range(4):
        hall[t, T : T + 128, 64 * q : 64 * q + 64] = hid_ref[128 * q : 128 * q + 128, 256:320]
    own_w = pl.ds(pl.multiple_of(s * WR, 16), WR)
    wall[own_w, 0:512] = wq_ref[...].astype(jnp.bfloat16)
    wall[own_w, 512:640] = wk_ref[...].astype(jnp.bfloat16)
    wall[own_w, 640:768] = wv_ref[...].astype(jnp.bfloat16)

    pl.semaphore_wait(barrier, 7)

    started = []

    class Gather:
        def __init__(self, region, send, recv):
            self.region, self.send, self.recv, self.sends = region, send, recv, 0

        def go(self, rank, half, role, peer):
            ref = self.region(rank, half)
            copy = pltpu.make_async_remote_copy(
                src_ref=ref,
                dst_ref=ref,
                send_sem=self.send.at[self.sends],
                recv_sem=self.recv.at[role],
                device_id=peer,
                device_id_type=MESH,
            )
            self.sends += 1
            copy.start()
            started.append(copy)

        def wait(self, rank, half, role):
            ref = self.region(rank, half)
            pltpu.make_async_remote_copy(
                src_ref=ref,
                dst_ref=ref,
                send_sem=self.send.at[0],
                recv_sem=self.recv.at[role],
                device_id=sib,
                device_id_type=MESH,
            ).wait_recv()

    def h_region(rank, half):
        if half is None:
            return hall.at[rank]
        return hall.at[rank, pl.ds(half * (HR // 2), HR // 2), :]

    def w_region(rank, half):
        if half is None:
            return wall.at[pl.ds(pl.multiple_of(rank * WR, 16), WR), :]
        return wall.at[pl.ds(pl.multiple_of(rank * WR + half * (WR // 2), 16), WR // 2), :]

    def kv_region(rank, half):
        if half is None:
            return kv.at[pl.ds(rank * 8, 8)]
        return kv.at[pl.ds(rank * 8 + half * 4, 4)]

    seq_roles = [(0, 1, None), (3, 0, None), (3, 1, None), (1, 0, None), (1, 1, None), (2, 0, 0), (2, 1, 0), (2, 0, 1), (2, 1, 1)]
    seq_forward = {
        0: ((None, 2, xp), (None, 4, xm)),
        1: ((0, 5, xp),),
        2: ((0, 6, xp),),
        3: ((1, 7, xm),),
        4: ((1, 8, xm),),
    }

    def seq_begin(g):
        rank = seq_rank(0, 0, 0)
        g.go(rank, None, 0, yhp)
        g.go(rank, None, 1, xp)
        g.go(rank, None, 3, xm)
        g.go(rank, None, 10, sib)

    def seq_pass(g, role):
        dx, dy, half = seq_roles[role]
        rank = seq_rank(dx, dy, 0)
        g.wait(rank, half, role)
        for part, to, peer in seq_forward.get(role, ()):
            g.go(rank, part, to, peer)
        g.go(rank, half, 11 + role, sib)

    def seq_sib(g, role):
        if role is None:
            g.wait(seq_rank(0, 0, 1), None, 10)
        else:
            dx, dy, half = seq_roles[role]
            g.wait(seq_rank(dx, dy, 1), half, 11 + role)

    tp_roles = [(0, 1, None), (3, 0, None), (3, 1, None), (1, 0, None), (1, 1, None), (2, 0, 0), (2, 0, 1), (2, 1, 0), (2, 1, 1)]
    tp_forward = {
        0: ((None, 2, zp), (None, 4, zm)),
        1: ((0, 5, zp),),
        3: ((1, 6, zm),),
        5: ((0, 7, ylp),),
        6: ((1, 8, ylp),),
    }

    def tp_pass(g, role):
        dz, dy, half = tp_roles[role]
        rank = tp_rank(dz, dy)
        g.wait(rank, half, role)
        for part, to, peer in tp_forward.get(role, ()):
            g.go(rank, part, to, peer)

    gh = Gather(h_region, h_send, h_recv)
    gw = Gather(w_region, w_send, w_recv)
    gk = Gather(kv_region, kv_send, kv_recv)

    gh.go(t, None, 0, ylp)
    gh.go(t, None, 1, zp)
    gh.go(t, None, 3, zm)
    seq_begin(gw)

    def start_of(slots):
        start = jnp.zeros_like(slots)
        end = jnp.int32(0)
        for i in range(NSEG):
            end = end + len_ref[i]
            start = jnp.where(slots >= end, end, start)
        return start

    rows = s * T + lax.broadcasted_iota(jnp.int32, (T, HD), 0)
    position = (rows - start_of(rows)).astype(jnp.float32)
    angles = position * freq_ref[...]
    cosr[...] = jnp.cos(angles)
    lane = lax.broadcasted_iota(jnp.int32, (T, HD), 1)
    sine = jnp.sin(angles)
    sinr[...] = jnp.where(lane < HD // 2, -sine, sine)
    slots = s * T + lax.broadcasted_iota(jnp.int32, (8, T), 1)
    startr[...] = start_of(slots)
    label = lax.broadcasted_iota(jnp.int32, (HD, T), 0)
    lane_label = lax.broadcasted_iota(jnp.int32, (8, HD), 1)
    query_slot = s * T + lax.broadcasted_iota(jnp.int32, (HD, T), 1)
    mine = label >= NSEG
    low = jnp.zeros((8, HD), jnp.int32)
    high = jnp.zeros((8, HD), jnp.int32)
    end = jnp.int32(0)
    for i in range(NSEG):
        begin, end = end, end + len_ref[i]
        mine = mine | ((label == i) & (query_slot >= begin) & (query_slot < end))
        low = jnp.where(lane_label == i, begin, low)
        high = jnp.where(lane_label == i, end, high)
    other[...] = jnp.where(mine, 0.0, EXCLUDED).astype(jnp.bfloat16)
    bounds[0:1, :] = low[0:1, :]
    bounds[1:2, :] = high[0:1, :]

    per = T // PAGE
    source = [jnp.int32(0)] * per
    for b in range(PAGES):
        page = pt_ref[b] - s * per
        row = (b // per) * 2 * per + b % per
        source = [jnp.where(page == i, row, f) for i, f in enumerate(source)]

    ssq[...] = jnp.zeros_like(ssq)

    def add_squares(rank):
        v = hall[rank, 0:T, :].astype(jnp.float32)
        v = v * v
        ssq[...] += v[:, 0:HD] + v[:, HD:]

    add_squares(t)
    tp_pass(gh, 0)
    seq_pass(gw, 0)
    tp_pass(gh, 1)
    tp_pass(gh, 3)
    seq_pass(gw, 1)
    seq_pass(gw, 3)
    seq_sib(gw, None)
    tp_pass(gh, 5)
    tp_pass(gh, 6)
    seq_pass(gw, 2)
    seq_pass(gw, 4)
    for dz, dy in ((0, 1), (1, 0), (3, 0), (2, 0)):
        add_squares(tp_rank(dz, dy))
    for role in (5, 7, 6, 8):
        seq_pass(gw, role)
    for role in range(9):
        seq_sib(gw, role)
    tp_pass(gh, 2)
    add_squares(tp_rank(3, 1))
    tp_pass(gh, 4)
    add_squares(tp_rank(1, 1))
    tp_pass(gh, 7)
    tp_pass(gh, 8)
    add_squares(tp_rank(2, 1))

    half_lane = lax.broadcasted_iota(jnp.int32, (128, 128), 1) < 64
    for pair in range(TP // 2):
        for col in range(2):
            lanes = slice(128 * col, 128 * col + 128)
            a = hall[2 * pair, T : T + 128, lanes].astype(jnp.float32)
            b = hall[2 * pair + 1, T : T + 128, lanes].astype(jnp.float32)
            low = jnp.where(half_lane, a, pltpu.roll(b, 64, 1))
            high = jnp.where(half_lane, pltpu.roll(a, 64, 1), b)
            for q, v in ((2 * col, low), (2 * col + 1, high)):
                where = slice(128 * q, 128 * q + 128)
                ssq[where, :] += v * v
                hn[where, 2048 + 128 * pair : 2176 + 128 * pair] = v.astype(jnp.bfloat16)

    scale = lax.rsqrt(jnp.sum(ssq[...], axis=1, keepdims=True) * (1.0 / D) + EPS)
    for i in range(TP):
        v = hall[i, 0:T, :].astype(jnp.float32) * scale
        hn[:, 256 * i : 256 * i + 256] = (v * gain_ref[:, 256 * i : 256 * i + 256]).astype(jnp.bfloat16)
    v = hn[:, 2048:].astype(jnp.float32) * scale
    hn[:, 2048:] = (v * gain_ref[:, 2048:]).astype(jnp.bfloat16)

    def project(lo, hi):
        total = None
        for i in range(TP):
            w = wall[F * i : F * i + 256, lo:hi]
            part = jnp.dot(hn[:, 256 * i : 256 * i + 256], w, preferred_element_type=jnp.float32)
            total = part if total is None else total + part
        for i in range(2):
            w = jnp.concatenate([wall[F * j + 256 : F * j + 320, lo:hi] for j in range(4 * i, 4 * i + 4)], axis=0)
            at = 2048 + 256 * i
            total = total + jnp.dot(hn[:, at : at + 256], w, preferred_element_type=jnp.float32)
        return total

    def norm_rotate(u, gain):
        mean = jnp.sum(u * u, axis=1, keepdims=True) * (1.0 / HD)
        u = u * lax.rsqrt(mean + EPS) * gain
        return u * cosr[...] + pltpu.roll(u, HD // 2, 1) * sinr[...]

    kvp = project(512, 768)
    keys = norm_rotate(kvp[:, 0:HD], kg_ref[...]).astype(jnp.bfloat16)
    vt = kvp[:, HD:].T.astype(jnp.bfloat16)
    for i in range(T // PAGE):
        kv[s * 8 + i] = keys[PAGE * i : PAGE * i + PAGE, :]
        kv[s * 8 + per + i] = vt[:, PAGE * i : PAGE * i + PAGE]
    seq_begin(gk)

    for pair in range(G // 2):
        qp = project(256 * pair, 256 * pair + 256)
        for i in range(2):
            u = norm_rotate(qp[:, HD * i : HD * i + HD], qg_ref[...]).astype(jnp.bfloat16)
            qt[2 * pair + i] = u.astype(jnp.float32).T.astype(jnp.bfloat16)

    ones = jnp.where(lax.broadcasted_iota(jnp.int32, (VE - HD, T), 0) == 0, 1.0, 0.0).astype(jnp.bfloat16)

    def attend(rank, diagonal):
        keys = jnp.concatenate([kv[rank * 8 + i] for i in range(per)], axis=0)
        vals = jnp.concatenate([kv[rank * 8 + per + i] for i in range(per)], axis=1)
        vals = jnp.concatenate([vals, ones], axis=0)
        if not diagonal:
            key_slot = rank * T + lax.broadcasted_iota(jnp.int32, (T, HD), 0)
            member = (key_slot >= bounds[0:1, :]) & (key_slot < bounds[1:2, :])
            keys = jnp.concatenate([keys, jnp.where(member, 1.0, 0.0).astype(jnp.bfloat16)], axis=1)

        def score(h):
            if diagonal:
                return jnp.dot(keys, qt[h], preferred_element_type=jnp.float32)
            queries = jnp.concatenate([qt[h], other[...]], axis=0)
            return jnp.dot(keys, queries, preferred_element_type=jnp.float32)

        ahead = score(0)
        for h in range(G):
            scores = ahead
            if h + 1 < G:
                ahead = score(h + 1)
            if diagonal:
                key_slot = rank * T + lax.broadcasted_iota(jnp.int32, (T, T), 0)
                query_slot = rank * T + lax.broadcasted_iota(jnp.int32, (T, T), 1)
                allowed = (key_slot >= startr[0:1, :]) & (key_slot <= query_slot)
                scores = jnp.where(allowed, scores, EXCLUDED)
            top = jnp.max(scores, axis=0, keepdims=True)
            if not diagonal:
                old = mx[h]
                top = jnp.maximum(old, top)
            probs = jnp.exp2((scores - top) * SCALE).astype(jnp.bfloat16)
            sums = jnp.dot(vals, probs, preferred_element_type=jnp.float32)
            if diagonal:
                acc[h] = sums
            else:
                acc[h] = acc[h] * jnp.exp2((old - top) * SCALE) + sums
            mx[h] = top

    def attend_all(offsets):
        def one(k, carry):
            rank = seq_rank(*offsets[0])
            for i in range(1, len(offsets)):
                rank = jnp.where(k == i, seq_rank(*offsets[i]), rank)

            @pl.when((rank < s) & (rank + 8 >= s))
            def _():
                attend(rank, False)

            return carry

        lax.fori_loop(0, len(offsets), one, 0)

    attend(s, True)
    seq_pass(gk, 0)
    seq_pass(gk, 1)
    seq_pass(gk, 3)
    seq_sib(gk, None)
    attend_all([(0, 0, 1), (3, 0, 0), (1, 0, 0), (0, 1, 0)])
    seq_pass(gk, 2)
    seq_pass(gk, 4)
    for role in (0, 1, 3):
        seq_sib(gk, role)
    attend_all([(3, 0, 1), (1, 0, 1), (0, 1, 1), (3, 1, 0), (1, 1, 0)])
    for role in (5, 7, 6, 8):
        seq_pass(gk, role)
    for role in (2, 4):
        seq_sib(gk, role)
    attend_all([(3, 1, 1), (1, 1, 1), (2, 0, 0), (2, 1, 0)])
    for role in (5, 6, 7, 8):
        seq_sib(gk, role)
    attend_all([(2, 0, 1), (2, 1, 1)])

    for h in range(G):
        o = acc[h, 0:HD, :] / acc[h, HD : HD + 1, :]
        out_ref[:, HD * h : HD * h + HD] = o.T.astype(jnp.bfloat16)

    for i in range(per):
        kc_ref[i, 0] = kv[source[i]]
        page = kv[source[i] + per]
        vc_ref[i, 0] = page.astype(jnp.float32).T.astype(jnp.bfloat16)

    for copy in started:
        copy.wait_send()


def shards(hidden, norm_gain, query_weight, key_weight, value_weight, query_gain, key_gain, lengths, page_table):
    by_shard = norm_gain.reshape(TP, F)
    gain = jnp.concatenate([by_shard[:, :256].reshape(1, -1), by_shard[:, 256:].reshape(1, -1)], axis=1)
    half = 1000000.0 ** -(np.arange(HD // 2, dtype=np.float32) * np.float32(2.0 / HD))
    freq = jnp.asarray(np.concatenate([half, half])[None, :].astype(np.float32))
    vmem = pl.BlockSpec(memory_space=pltpu.VMEM)
    smem = pl.BlockSpec(memory_space=pltpu.SMEM)
    return pl.pallas_call(
        kernel,
        out_shape=(
            jax.ShapeDtypeStruct((T, G * HD), jnp.bfloat16),
            jax.ShapeDtypeStruct((T // PAGE, 1, PAGE, HD), jnp.bfloat16),
            jax.ShapeDtypeStruct((T // PAGE, 1, PAGE, HD), jnp.bfloat16),
        ),
        in_specs=[vmem] * 8 + [smem] * 2,
        out_specs=(vmem,) * 3,
        scratch_shapes=[
            pltpu.VMEM((TP, HR, 256), jnp.bfloat16),
            pltpu.VMEM((D, NC), jnp.bfloat16),
            pltpu.VMEM((SEQ * 8, PAGE, HD), jnp.bfloat16),
            pltpu.VMEM((T, D), jnp.bfloat16),
            pltpu.VMEM((G, HD, T), jnp.bfloat16),
            pltpu.VMEM((G, VE, T), jnp.float32),
            pltpu.VMEM((G, 1, T), jnp.float32),
            pltpu.VMEM((T, HD), jnp.float32),
            pltpu.VMEM((T, HD), jnp.float32),
            pltpu.VMEM((8, T), jnp.int32),
            pltpu.VMEM((HD, T), jnp.bfloat16),
            pltpu.VMEM((8, HD), jnp.int32),
            pltpu.VMEM((T, HD), jnp.float32),
            pltpu.SemaphoreType.DMA((9,)),
            pltpu.SemaphoreType.DMA((9,)),
            pltpu.SemaphoreType.DMA((20,)),
            pltpu.SemaphoreType.DMA((20,)),
            pltpu.SemaphoreType.DMA((20,)),
            pltpu.SemaphoreType.DMA((20,)),
        ],
        compiler_params=pltpu.CompilerParams(
            collective_id=0, has_side_effects=True, vmem_limit_bytes=48 * 1024 * 1024
        ),
        cost_estimate=pl.CostEstimate(flops=7 * 10**9, bytes_accessed=4 * 10**6, transcendentals=10**7),
    )(
        hidden,
        gain,
        query_weight,
        key_weight,
        value_weight,
        query_gain.reshape(1, HD),
        key_gain.reshape(1, HD),
        freq,
        lengths,
        page_table,
    )


def solution(mesh):
    return jax.shard_map(
        shards,
        mesh=mesh,
        in_specs=(
            P("seq", "tp"),
            P(),
            P("seq", "tp"),
            P("seq", "tp"),
            P("seq", "tp"),
            P(),
            P(),
            P(),
            P(),
        ),
        out_specs=(P("seq", "tp"), P("seq", "tp", None, None), P("seq", "tp", None, None)),
        check_vma=False,
    )
```

```python
import math

import jax
import jax.numpy as jnp
import numpy as np
from jax import lax
from jax.experimental import pallas as pl
from jax.experimental.pallas import tpu as pltpu
from jax.sharding import PartitionSpec as P

T = 512
F = 320
D = 2560
WR = 160
HD = 128
G = 4
NC = 768
PAGE = 128
PAGES = 64
NSEG = 8
SEQ = 16
TP = 8
EPS = 1e-6
EXCLUDED = -1e30
HR = 640
MESH = pl.DeviceIdType.MESH
SCALE = HD**-0.5 * math.log2(math.e)
VE = HD + 16


def kernel(
    hid_ref,
    gain_1d,
    wq_ref,
    wk_ref,
    wv_ref,
    qg_ref,
    kg_ref,
    freq_ref,
    len_ref,
    pt_ref,
    out_ref,
    kc_ref,
    vc_ref,
    hall,
    wall,
    kv,
    hn,
    qt,
    acc,
    mx,
    cosr,
    sinr,
    startr,
    other,
    bounds,
    ssq,
    h_send,
    h_recv,
    w_send,
    w_recv,
    kv_send,
    kv_recv,
):
    s = lax.axis_index("seq")
    t = lax.axis_index("tp")
    yh, x, c = s // 8, (s // 2) % 4, s % 2
    yl, z = t // 4, t % 4

    def seq_rank(dx, dy, dc):
        return ((yh + dy) % 2) * 8 + ((x + dx) % 4) * 2 + (c + dc) % 2

    def tp_rank(dz, dy):
        return ((yl + dy) % 2) * 4 + (z + dz) % 4

    sib = {"seq": seq_rank(0, 0, 1), "tp": t}
    xp = {"seq": seq_rank(1, 0, 0), "tp": t}
    xm = {"seq": seq_rank(3, 0, 0), "tp": t}
    yhp = {"seq": seq_rank(0, 1, 0), "tp": t}
    zp = {"seq": s, "tp": tp_rank(1, 0)}
    zm = {"seq": s, "tp": tp_rank(3, 0)}
    ylp = {"seq": s, "tp": tp_rank(0, 1)}
    barrier = pltpu.get_barrier_semaphore()
    for peer in (sib, xp, xm, yhp, zp, zm, ylp):
        pl.semaphore_signal(barrier, inc=1, device_id=peer, device_id_type=MESH)

    hall[t, 0:T, :] = hid_ref[:, 0:256]
    for q in range(4):
        hall[t, T : T + 128, 64 * q : 64 * q + 64] = hid_ref[128 * q : 128 * q + 128, 256:320]
    own_w = pl.ds(pl.multiple_of(s * WR, 16), WR)
    wall[own_w, 0:512] = wq_ref[...].astype(jnp.bfloat16)
    wall[own_w, 512:640] = wk_ref[...].astype(jnp.bfloat16)
    wall[own_w, 640:768] = wv_ref[...].astype(jnp.bfloat16)

    pl.semaphore_wait(barrier, 7)

    started = []

    class Gather:
        def __init__(self, region, send, recv):
            self.region, self.send, self.recv, self.sends = region, send, recv, 0

        def go(self, rank, half, role, peer):
            ref = self.region(rank, half)
            copy = pltpu.make_async_remote_copy(
                src_ref=ref,
                dst_ref=ref,
                send_sem=self.send.at[self.sends],
                recv_sem=self.recv.at[role],
                device_id=peer,
                device_id_type=MESH,
            )
            self.sends += 1
            copy.start()
            started.append(copy)

        def wait(self, rank, half, role):
            ref = self.region(rank, half)
            pltpu.make_async_remote_copy(
                src_ref=ref,
                dst_ref=ref,
                send_sem=self.send.at[0],
                recv_sem=self.recv.at[role],
                device_id=sib,
                device_id_type=MESH,
            ).wait_recv()

    def h_region(rank, half):
        if half is None:
            return hall.at[rank]
        return hall.at[rank, pl.ds(half * (HR // 2), HR // 2), :]

    def w_region(rank, half):
        if half is None:
            return wall.at[pl.ds(pl.multiple_of(rank * WR, 16), WR), :]
        return wall.at[pl.ds(pl.multiple_of(rank * WR + half * (WR // 2), 16), WR // 2), :]

    def kv_region(rank, half):
        if half is None:
            return kv.at[pl.ds(rank * 8, 8)]
        return kv.at[pl.ds(rank * 8 + half * 4, 4)]

    seq_roles = [(0, 1, None), (3, 0, None), (3, 1, None), (1, 0, None), (1, 1, None), (2, 0, 0), (2, 1, 0), (2, 0, 1), (2, 1, 1)]
    seq_forward = {
        0: ((None, 2, xp), (None, 4, xm)),
        1: ((0, 5, xp),),
        2: ((0, 6, xp),),
        3: ((1, 7, xm),),
        4: ((1, 8, xm),),
    }

    def seq_begin(g):
        rank = seq_rank(0, 0, 0)
        g.go(rank, None, 0, yhp)
        g.go(rank, None, 1, xp)
        g.go(rank, None, 3, xm)
        g.go(rank, None, 10, sib)

    def seq_pass(g, role):
        dx, dy, half = seq_roles[role]
        rank = seq_rank(dx, dy, 0)
        g.wait(rank, half, role)
        for part, to, peer in seq_forward.get(role, ()):
            g.go(rank, part, to, peer)
        g.go(rank, half, 11 + role, sib)

    def seq_sib(g, role):
        if role is None:
            g.wait(seq_rank(0, 0, 1), None, 10)
        else:
            dx, dy, half = seq_roles[role]
            g.wait(seq_rank(dx, dy, 1), half, 11 + role)

    tp_roles = {"zm": (3, 0), "zp": (1, 0), "y": (0, 1), "z2": (2, 0), "zmy": (3, 1), "zpy": (1, 1), "z2y": (2, 1)}
    tp_index = {name: 2 * i for i, name in enumerate(tp_roles)}
    tp_forward = {
        ("zm", 0): (("z2", zp),),
        ("zp", 1): (("z2", zm),),
        ("y", 0): (("zmy", zp), ("zpy", zm)),
        ("y", 1): (("zmy", zp), ("zpy", zm)),
        ("z2", 0): (("z2y", ylp),),
        ("z2", 1): (("z2y", ylp),),
    }

    def tp_pass(name, piece):
        rank = tp_rank(*tp_roles[name])
        gh.wait(rank, piece, tp_index[name] + piece)
        for to, peer in tp_forward.get((name, piece), ()):
            gh.go(rank, piece, tp_index[to] + piece, peer)

    def tp_begin(name, piece, peer):
        gh.go(t, piece, tp_index[name] + piece, peer)

    gh = Gather(h_region, h_send, h_recv)
    gw = Gather(w_region, w_send, w_recv)
    gk = Gather(kv_region, kv_send, kv_recv)

    tp_begin("zm", 0, zp)
    tp_begin("zp", 1, zm)
    tp_begin("y", 0, ylp)
    gw.go(s, None, 0, yhp)
    tp_begin("y", 1, ylp)
    gw.go(s, None, 1, xp)
    gw.go(s, None, 3, xm)
    tp_begin("zm", 1, zp)
    tp_begin("zp", 0, zm)
    gw.go(s, None, 10, sib)

    def start_of(slots):
        start = jnp.zeros_like(slots)
        end = jnp.int32(0)
        for i in range(NSEG):
            end = end + len_ref[i]
            start = jnp.where(slots >= end, end, start)
        return start

    rows = s * T + lax.broadcasted_iota(jnp.int32, (T, HD), 0)
    position = (rows - start_of(rows)).astype(jnp.float32)
    angles = position * freq_ref[...]
    cosr[...] = jnp.cos(angles)
    lane = lax.broadcasted_iota(jnp.int32, (T, HD), 1)
    sine = jnp.sin(angles)
    sinr[...] = jnp.where(lane < HD // 2, -sine, sine)
    slots = s * T + lax.broadcasted_iota(jnp.int32, (8, T), 1)
    startr[...] = start_of(slots)
    label = lax.broadcasted_iota(jnp.int32, (HD, T), 0)
    lane_label = lax.broadcasted_iota(jnp.int32, (8, HD), 1)
    query_slot = s * T + lax.broadcasted_iota(jnp.int32, (HD, T), 1)
    mine = label >= NSEG
    low = jnp.zeros((8, HD), jnp.int32)
    high = jnp.zeros((8, HD), jnp.int32)
    end = jnp.int32(0)
    for i in range(NSEG):
        begin, end = end, end + len_ref[i]
        mine = mine | ((label == i) & (query_slot >= begin) & (query_slot < end))
        low = jnp.where(lane_label == i, begin, low)
        high = jnp.where(lane_label == i, end, high)
    other[...] = jnp.where(mine, 0.0, EXCLUDED).astype(jnp.bfloat16)
    bounds[0:1, :] = low[0:1, :]
    bounds[1:2, :] = high[0:1, :]

    per = T // PAGE
    source = [jnp.int32(0)] * per
    for b in range(PAGES):
        page = pt_ref[b] - s * per
        row = (b // per) * 2 * per + b % per
        source = [jnp.where(page == i, row, f) for i, f in enumerate(source)]

    ssq[...] = jnp.zeros_like(ssq)

    def add_squares(rank):
        v = hall[rank, 0:T, :].astype(jnp.float32)
        v = v * v
        ssq[...] += v[:, 0:HD] + v[:, HD:]

    add_squares(t)
    for name, piece in (("zm", 0), ("zp", 1)):
        tp_pass(name, piece)
    seq_pass(gw, 1)
    seq_pass(gw, 3)
    for name, piece in (("zm", 1), ("zp", 0), ("y", 0)):
        tp_pass(name, piece)
    seq_pass(gw, 0)
    tp_pass("y", 1)
    tp_pass("z2", 0)
    seq_pass(gw, 5)
    tp_pass("z2", 1)
    seq_pass(gw, 7)
    for dz, dy in ((0, 1), (1, 0), (3, 0), (2, 0)):
        add_squares(tp_rank(dz, dy))
    seq_pass(gw, 2)
    seq_pass(gw, 4)
    for name, piece in (("zmy", 0), ("zpy", 0), ("zmy", 1), ("zpy", 1)):
        tp_pass(name, piece)
    seq_pass(gw, 6)
    seq_pass(gw, 8)
    add_squares(tp_rank(3, 1))
    add_squares(tp_rank(1, 1))
    tp_pass("z2y", 0)
    tp_pass("z2y", 1)
    add_squares(tp_rank(2, 1))
    seq_sib(gw, None)
    for role in range(9):
        seq_sib(gw, role)

    gain_row = gain_1d[...].reshape(1, D)
    gain_ref = [gain_row[:, F * i : F * i + 256] for i in range(TP)]
    gain_last = jnp.concatenate([gain_row[:, F * i + 256 : F * i + F] for i in range(TP)], axis=1)

    half_lane = lax.broadcasted_iota(jnp.int32, (128, 128), 1) < 64
    for pair in range(TP // 2):
        for col in range(2):
            lanes = slice(128 * col, 128 * col + 128)
            a = hall[2 * pair, T : T + 128, lanes].astype(jnp.float32)
            b = hall[2 * pair + 1, T : T + 128, lanes].astype(jnp.float32)
            low = jnp.where(half_lane, a, pltpu.roll(b, 64, 1))
            high = jnp.where(half_lane, pltpu.roll(a, 64, 1), b)
            for q, v in ((2 * col, low), (2 * col + 1, high)):
                where = slice(128 * q, 128 * q + 128)
                ssq[where, :] += v * v
                hn[where, 2048 + 128 * pair : 2176 + 128 * pair] = v.astype(jnp.bfloat16)

    scale = lax.rsqrt(jnp.sum(ssq[...], axis=1, keepdims=True) * (1.0 / D) + EPS)
    for i in range(TP):
        v = hall[i, 0:T, :].astype(jnp.float32) * scale
        hn[:, 256 * i : 256 * i + 256] = (v * gain_ref[i]).astype(jnp.bfloat16)
    v = hn[:, 2048:].astype(jnp.float32) * scale
    hn[:, 2048:] = (v * gain_last).astype(jnp.bfloat16)

    def project(lo, hi):
        total = None
        for i in range(TP):
            w = wall[F * i : F * i + 256, lo:hi]
            part = jnp.dot(hn[:, 256 * i : 256 * i + 256], w, preferred_element_type=jnp.float32)
            total = part if total is None else total + part
        for i in range(2):
            w = jnp.concatenate([wall[F * j + 256 : F * j + 320, lo:hi] for j in range(4 * i, 4 * i + 4)], axis=0)
            at = 2048 + 256 * i
            total = total + jnp.dot(hn[:, at : at + 256], w, preferred_element_type=jnp.float32)
        return total

    def norm_rotate(u, gain):
        mean = jnp.sum(u * u, axis=1, keepdims=True) * (1.0 / HD)
        u = u * lax.rsqrt(mean + EPS) * gain
        return u * cosr[...] + pltpu.roll(u, HD // 2, 1) * sinr[...]

    kvp = project(512, 768)
    keys = norm_rotate(kvp[:, 0:HD], kg_ref[...]).astype(jnp.bfloat16)
    vt = kvp[:, HD:].T.astype(jnp.bfloat16)
    for i in range(T // PAGE):
        kv[s * 8 + i] = keys[PAGE * i : PAGE * i + PAGE, :]
        kv[s * 8 + per + i] = vt[:, PAGE * i : PAGE * i + PAGE]
    seq_begin(gk)

    for pair in range(G // 2):
        qp = project(256 * pair, 256 * pair + 256)
        for i in range(2):
            u = norm_rotate(qp[:, HD * i : HD * i + HD], qg_ref[...]).astype(jnp.bfloat16)
            qt[2 * pair + i] = u.astype(jnp.float32).T.astype(jnp.bfloat16)

    ones = jnp.where(lax.broadcasted_iota(jnp.int32, (VE - HD, T), 0) == 0, 1.0, 0.0).astype(jnp.bfloat16)

    def attend(rank, diagonal):
        keys = jnp.concatenate([kv[rank * 8 + i] for i in range(per)], axis=0)
        vals = jnp.concatenate([kv[rank * 8 + per + i] for i in range(per)], axis=1)
        vals = jnp.concatenate([vals, ones], axis=0)
        if not diagonal:
            key_slot = rank * T + lax.broadcasted_iota(jnp.int32, (T, HD), 0)
            member = (key_slot >= bounds[0:1, :]) & (key_slot < bounds[1:2, :])
            keys = jnp.concatenate([keys, jnp.where(member, 1.0, 0.0).astype(jnp.bfloat16)], axis=1)

        def score(h):
            if diagonal:
                return jnp.dot(keys, qt[h], preferred_element_type=jnp.float32)
            queries = jnp.concatenate([qt[h], other[...]], axis=0)
            return jnp.dot(keys, queries, preferred_element_type=jnp.float32)

        ahead = score(0)
        for h in range(G):
            scores = ahead
            if h + 1 < G:
                ahead = score(h + 1)
            if diagonal:
                key_slot = rank * T + lax.broadcasted_iota(jnp.int32, (T, T), 0)
                query_slot = rank * T + lax.broadcasted_iota(jnp.int32, (T, T), 1)
                allowed = (key_slot >= startr[0:1, :]) & (key_slot <= query_slot)
                scores = jnp.where(allowed, scores, EXCLUDED)
            top = jnp.max(scores, axis=0, keepdims=True)
            if not diagonal:
                old = mx[h]
                top = jnp.maximum(old, top)
            probs = jnp.exp2((scores - top) * SCALE).astype(jnp.bfloat16)
            sums = jnp.dot(vals, probs, preferred_element_type=jnp.float32)
            if diagonal:
                acc[h] = sums
            else:
                acc[h] = acc[h] * jnp.exp2((old - top) * SCALE) + sums
            mx[h] = top

    def attend_all(offsets):
        def one(k, carry):
            rank = seq_rank(*offsets[0])
            for i in range(1, len(offsets)):
                rank = jnp.where(k == i, seq_rank(*offsets[i]), rank)

            @pl.when((rank < s) & (rank + 8 >= s))
            def _():
                attend(rank, False)

            return carry

        lax.fori_loop(0, len(offsets), one, 0)

    attend(s, True)
    seq_pass(gk, 0)
    seq_pass(gk, 1)
    seq_pass(gk, 3)
    seq_sib(gk, None)
    attend_all([(0, 0, 1), (0, 1, 0)])
    seq_pass(gk, 2)
    seq_pass(gk, 4)
    for role in (0, 1, 3):
        seq_sib(gk, role)
    attend_all([(3, 0, 0), (1, 0, 0), (0, 1, 1)])
    for role in (5, 7):
        seq_pass(gk, role)
    attend_all([(3, 0, 1), (1, 0, 1), (3, 1, 0), (1, 1, 0), (2, 0, 0)])
    for role in (6, 8):
        seq_pass(gk, role)
    for role in (2, 4, 5, 7):
        seq_sib(gk, role)
    attend_all([(3, 1, 1), (1, 1, 1), (2, 0, 1), (2, 1, 0)])
    for role in (6, 8):
        seq_sib(gk, role)
    attend_all([(2, 1, 1)])

    for h in range(G):
        o = acc[h, 0:HD, :] / acc[h, HD : HD + 1, :]
        out_ref[:, HD * h : HD * h + HD] = o.T.astype(jnp.bfloat16)

    for i in range(per):
        kc_ref[i, 0] = kv[source[i]]
        page = kv[source[i] + per]
        vc_ref[i, 0] = page.astype(jnp.float32).T.astype(jnp.bfloat16)

    for copy in started:
        copy.wait_send()


def shards(hidden, norm_gain, query_weight, key_weight, value_weight, query_gain, key_gain, lengths, page_table):
    half = 1000000.0 ** -(np.arange(HD // 2, dtype=np.float32) * np.float32(2.0 / HD))
    freq = jnp.asarray(np.concatenate([half, half])[None, :].astype(np.float32))
    vmem = pl.BlockSpec(memory_space=pltpu.VMEM)
    smem = pl.BlockSpec(memory_space=pltpu.SMEM)
    return pl.pallas_call(
        kernel,
        out_shape=(
            jax.ShapeDtypeStruct((T, G * HD), jnp.bfloat16),
            jax.ShapeDtypeStruct((T // PAGE, 1, PAGE, HD), jnp.bfloat16),
            jax.ShapeDtypeStruct((T // PAGE, 1, PAGE, HD), jnp.bfloat16),
        ),
        in_specs=[vmem] * 8 + [smem] * 2,
        out_specs=(vmem,) * 3,
        scratch_shapes=[
            pltpu.VMEM((TP, HR, 256), jnp.bfloat16),
            pltpu.VMEM((D, NC), jnp.bfloat16),
            pltpu.VMEM((SEQ * 8, PAGE, HD), jnp.bfloat16),
            pltpu.VMEM((T, D), jnp.bfloat16),
            pltpu.VMEM((G, HD, T), jnp.bfloat16),
            pltpu.VMEM((G, VE, T), jnp.float32),
            pltpu.VMEM((G, 1, T), jnp.float32),
            pltpu.VMEM((T, HD), jnp.float32),
            pltpu.VMEM((T, HD), jnp.float32),
            pltpu.VMEM((8, T), jnp.int32),
            pltpu.VMEM((HD, T), jnp.bfloat16),
            pltpu.VMEM((8, HD), jnp.int32),
            pltpu.VMEM((T, HD), jnp.float32),
            pltpu.SemaphoreType.DMA((14,)),
            pltpu.SemaphoreType.DMA((14,)),
            pltpu.SemaphoreType.DMA((20,)),
            pltpu.SemaphoreType.DMA((20,)),
            pltpu.SemaphoreType.DMA((20,)),
            pltpu.SemaphoreType.DMA((20,)),
        ],
        compiler_params=pltpu.CompilerParams(
            collective_id=0, has_side_effects=True, vmem_limit_bytes=48 * 1024 * 1024
        ),
        cost_estimate=pl.CostEstimate(flops=7 * 10**9, bytes_accessed=4 * 10**6, transcendentals=10**7),
    )(
        hidden,
        norm_gain,
        query_weight,
        key_weight,
        value_weight,
        query_gain.reshape(1, HD),
        key_gain.reshape(1, HD),
        freq,
        lengths,
        page_table,
    )


def solution(mesh):
    return jax.shard_map(
        shards,
        mesh=mesh,
        in_specs=(
            P("seq", "tp"),
            P(),
            P("seq", "tp"),
            P("seq", "tp"),
            P("seq", "tp"),
            P(),
            P(),
            P(),
            P(),
        ),
        out_specs=(P("seq", "tp"), P("seq", "tp", None, None), P("seq", "tp", None, None)),
        check_vma=False,
    )
```

```python
import math

import jax
import jax.numpy as jnp
import numpy as np
from jax import lax
from jax.experimental import pallas as pl
from jax.experimental.pallas import tpu as pltpu
from jax.sharding import PartitionSpec as P

T = 512
F = 320
D = 2560
WR = 160
HD = 128
G = 4
NC = 768
PAGE = 128
PAGES = 64
NSEG = 8
SEQ = 16
TP = 8
EPS = 1e-6
EXCLUDED = -1e30
HR = 640
MESH = pl.DeviceIdType.MESH
SCALE = HD**-0.5 * math.log2(math.e)
VE = HD + 16


def kernel(
    hid_ref,
    gain_1d,
    wq_ref,
    wk_ref,
    wv_ref,
    qg_ref,
    kg_ref,
    freq_ref,
    len_ref,
    pt_ref,
    out_ref,
    kc_ref,
    vc_ref,
    hall,
    wall,
    kv,
    hn,
    qt,
    acc,
    mx,
    cosr,
    sinr,
    startr,
    other,
    bounds,
    ssq,
    h_send,
    h_recv,
    w_send,
    w_recv,
    kv_send,
    kv_recv,
):
    s = lax.axis_index("seq")
    t = lax.axis_index("tp")
    yh, x, c = s // 8, (s // 2) % 4, s % 2
    yl, z = t // 4, t % 4

    def seq_rank(dx, dy, dc):
        return ((yh + dy) % 2) * 8 + ((x + dx) % 4) * 2 + (c + dc) % 2

    def tp_rank(dz, dy):
        return ((yl + dy) % 2) * 4 + (z + dz) % 4

    sib = {"seq": seq_rank(0, 0, 1), "tp": t}
    xp = {"seq": seq_rank(1, 0, 0), "tp": t}
    xm = {"seq": seq_rank(3, 0, 0), "tp": t}
    yhp = {"seq": seq_rank(0, 1, 0), "tp": t}
    zp = {"seq": s, "tp": tp_rank(1, 0)}
    zm = {"seq": s, "tp": tp_rank(3, 0)}
    ylp = {"seq": s, "tp": tp_rank(0, 1)}
    barrier = pltpu.get_barrier_semaphore()
    for peer in (sib, xp, xm, yhp, zp, zm, ylp):
        pl.semaphore_signal(barrier, inc=1, device_id=peer, device_id_type=MESH)

    hall[t, 0:T, :] = hid_ref[:, 0:256]
    for q in range(4):
        hall[t, T : T + 128, 64 * q : 64 * q + 64] = hid_ref[128 * q : 128 * q + 128, 256:320]
    own_w = pl.ds(pl.multiple_of(s * WR, 16), WR)
    wall[own_w, 0:512] = wq_ref[...].astype(jnp.bfloat16)
    wall[own_w, 512:640] = wk_ref[...].astype(jnp.bfloat16)
    wall[own_w, 640:768] = wv_ref[...].astype(jnp.bfloat16)

    pl.semaphore_wait(barrier, 7)

    started = []

    class Gather:
        def __init__(self, region, send, recv):
            self.region, self.send, self.recv, self.sends = region, send, recv, 0

        def go(self, rank, half, role, peer):
            ref = self.region(rank, half)
            copy = pltpu.make_async_remote_copy(
                src_ref=ref,
                dst_ref=ref,
                send_sem=self.send.at[self.sends],
                recv_sem=self.recv.at[role],
                device_id=peer,
                device_id_type=MESH,
            )
            self.sends += 1
            copy.start()
            started.append(copy)

        def wait(self, rank, half, role):
            ref = self.region(rank, half)
            pltpu.make_async_remote_copy(
                src_ref=ref,
                dst_ref=ref,
                send_sem=self.send.at[0],
                recv_sem=self.recv.at[role],
                device_id=sib,
                device_id_type=MESH,
            ).wait_recv()

    def h_region(rank, half):
        if half is None:
            return hall.at[rank]
        return hall.at[rank, pl.ds(half * (HR // 2), HR // 2), :]

    def w_region(rank, half):
        if half is None:
            return wall.at[pl.ds(pl.multiple_of(rank * WR, 16), WR), :]
        return wall.at[pl.ds(pl.multiple_of(rank * WR + half * (WR // 2), 16), WR // 2), :]

    def kv_region(rank, half):
        if half is None:
            return kv.at[pl.ds(rank * 8, 8)]
        return kv.at[pl.ds(rank * 8 + half * 4, 4)]

    seq_roles = [(0, 1, None), (3, 0, None), (3, 1, None), (1, 0, None), (1, 1, None), (2, 0, 0), (2, 1, 0), (2, 0, 1), (2, 1, 1)]
    seq_forward = {
        0: ((None, 2, xp), (None, 4, xm)),
        1: ((0, 5, xp),),
        2: ((0, 6, xp),),
        3: ((1, 7, xm),),
        4: ((1, 8, xm),),
    }

    def seq_pass(g, role):
        dx, dy, half = seq_roles[role]
        rank = seq_rank(dx, dy, 0)
        g.wait(rank, half, role)
        for part, to, peer in seq_forward.get(role, ()):
            g.go(rank, part, to, peer)
        g.go(rank, half, 11 + role, sib)

    def seq_sib(g, role):
        if role is None:
            g.wait(seq_rank(0, 0, 1), None, 10)
        else:
            dx, dy, half = seq_roles[role]
            g.wait(seq_rank(dx, dy, 1), half, 11 + role)

    tp_roles = {"zm": (3, 0), "zp": (1, 0), "y": (0, 1), "z2": (2, 0), "zmy": (3, 1), "zpy": (1, 1), "z2y": (2, 1)}
    tp_index = {name: 2 * i for i, name in enumerate(tp_roles)}
    tp_forward = {
        ("zm", 0): (("z2", zp),),
        ("zp", 1): (("z2", zm),),
        ("y", 0): (("zmy", zp), ("zpy", zm)),
        ("y", 1): (("zmy", zp), ("zpy", zm)),
        ("z2", 0): (("z2y", ylp),),
        ("z2", 1): (("z2y", ylp),),
    }

    def tp_pass(name, piece):
        rank = tp_rank(*tp_roles[name])
        gh.wait(rank, piece, tp_index[name] + piece)
        for to, peer in tp_forward.get((name, piece), ()):
            gh.go(rank, piece, tp_index[to] + piece, peer)

    def tp_begin(name, piece, peer):
        gh.go(t, piece, tp_index[name] + piece, peer)

    kv_roles = {"xm": (3, 0), "xp": (1, 0), "y": (0, 1), "x2": (2, 0), "xmy": (3, 1), "xpy": (1, 1), "x2y": (2, 1)}
    kv_index = {name: i for i, name in enumerate(kv_roles)}
    kv_forward = {
        ("xm", 0): (("x2", xp),),
        ("xp", 1): (("x2", xm),),
        ("y", 0): (("xmy", xp), ("xpy", xm)),
        ("y", 1): (("xmy", xp), ("xpy", xm)),
        ("x2", 0): (("x2y", yhp),),
        ("x2", 1): (("x2y", yhp),),
    }

    def kv_begin():
        for name, piece, peer in (("xm", 0, xp), ("xp", 1, xm), ("y", 0, yhp), ("y", 1, yhp), ("xm", 1, xp), ("xp", 0, xm)):
            gk.go(s, piece, 2 * kv_index[name] + piece, peer)
        gk.go(s, None, 21, sib)

    def kv_pass(name, piece):
        rank = seq_rank(*kv_roles[name], 0)
        gk.wait(rank, piece, 2 * kv_index[name] + piece)
        for to, peer in kv_forward.get((name, piece), ()):
            gk.go(rank, piece, 2 * kv_index[to] + piece, peer)

    def kv_share(name):
        gk.go(seq_rank(*kv_roles[name], 0), None, 14 + kv_index[name], sib)

    def kv_sib(name):
        gk.wait(seq_rank(*kv_roles[name], 1), None, 14 + kv_index[name])

    gh = Gather(h_region, h_send, h_recv)
    gw = Gather(w_region, w_send, w_recv)
    gk = Gather(kv_region, kv_send, kv_recv)

    tp_begin("zm", 0, zp)
    tp_begin("zp", 1, zm)
    tp_begin("y", 0, ylp)
    gw.go(s, None, 0, yhp)
    tp_begin("y", 1, ylp)
    gw.go(s, None, 1, xp)
    gw.go(s, None, 3, xm)
    tp_begin("zm", 1, zp)
    tp_begin("zp", 0, zm)
    gw.go(s, None, 10, sib)

    def start_of(slots):
        start = jnp.zeros_like(slots)
        end = jnp.int32(0)
        for i in range(NSEG):
            end = end + len_ref[i]
            start = jnp.where(slots >= end, end, start)
        return start

    rows = s * T + lax.broadcasted_iota(jnp.int32, (T, HD), 0)
    position = (rows - start_of(rows)).astype(jnp.float32)
    angles = position * freq_ref[...]
    cosr[...] = jnp.cos(angles)
    lane = lax.broadcasted_iota(jnp.int32, (T, HD), 1)
    sine = jnp.sin(angles)
    sinr[...] = jnp.where(lane < HD // 2, -sine, sine)
    slots = s * T + lax.broadcasted_iota(jnp.int32, (8, T), 1)
    startr[...] = start_of(slots)
    label = lax.broadcasted_iota(jnp.int32, (HD, T), 0)
    lane_label = lax.broadcasted_iota(jnp.int32, (8, HD), 1)
    query_slot = s * T + lax.broadcasted_iota(jnp.int32, (HD, T), 1)
    mine = label >= NSEG
    low = jnp.zeros((8, HD), jnp.int32)
    high = jnp.zeros((8, HD), jnp.int32)
    end = jnp.int32(0)
    for i in range(NSEG):
        begin, end = end, end + len_ref[i]
        mine = mine | ((label == i) & (query_slot >= begin) & (query_slot < end))
        low = jnp.where(lane_label == i, begin, low)
        high = jnp.where(lane_label == i, end, high)
    other[...] = jnp.where(mine, 0.0, EXCLUDED).astype(jnp.bfloat16)
    bounds[0:1, :] = low[0:1, :]
    bounds[1:2, :] = high[0:1, :]

    per = T // PAGE
    source = [jnp.int32(0)] * per
    for b in range(PAGES):
        page = pt_ref[b] - s * per
        row = (b // per) * 2 * per + b % per
        source = [jnp.where(page == i, row, f) for i, f in enumerate(source)]

    ssq[...] = jnp.zeros_like(ssq)

    def add_squares(rank):
        v = hall[rank, 0:T, :].astype(jnp.float32)
        v = v * v
        ssq[...] += v[:, 0:HD] + v[:, HD:]

    add_squares(t)
    for name, piece in (("zm", 0), ("zp", 1)):
        tp_pass(name, piece)
    seq_pass(gw, 1)
    seq_pass(gw, 3)
    for name, piece in (("zm", 1), ("zp", 0), ("y", 0)):
        tp_pass(name, piece)
    seq_pass(gw, 0)
    tp_pass("y", 1)
    tp_pass("z2", 0)
    seq_pass(gw, 5)
    tp_pass("z2", 1)
    seq_pass(gw, 7)
    for dz, dy in ((0, 1), (1, 0), (3, 0), (2, 0)):
        add_squares(tp_rank(dz, dy))
    seq_pass(gw, 2)
    seq_pass(gw, 4)
    for name, piece in (("zmy", 0), ("zpy", 0), ("zmy", 1), ("zpy", 1)):
        tp_pass(name, piece)
    seq_pass(gw, 6)
    seq_pass(gw, 8)
    add_squares(tp_rank(3, 1))
    add_squares(tp_rank(1, 1))
    tp_pass("z2y", 0)
    tp_pass("z2y", 1)
    add_squares(tp_rank(2, 1))
    seq_sib(gw, None)
    for role in range(9):
        seq_sib(gw, role)

    gain_row = gain_1d[...].reshape(1, D)
    gain_ref = [gain_row[:, F * i : F * i + 256] for i in range(TP)]
    gain_last = jnp.concatenate([gain_row[:, F * i + 256 : F * i + F] for i in range(TP)], axis=1)

    half_lane = lax.broadcasted_iota(jnp.int32, (128, 128), 1) < 64
    for pair in range(TP // 2):
        for col in range(2):
            lanes = slice(128 * col, 128 * col + 128)
            a = hall[2 * pair, T : T + 128, lanes].astype(jnp.float32)
            b = hall[2 * pair + 1, T : T + 128, lanes].astype(jnp.float32)
            low = jnp.where(half_lane, a, pltpu.roll(b, 64, 1))
            high = jnp.where(half_lane, pltpu.roll(a, 64, 1), b)
            for q, v in ((2 * col, low), (2 * col + 1, high)):
                where = slice(128 * q, 128 * q + 128)
                ssq[where, :] += v * v
                hn[where, 2048 + 128 * pair : 2176 + 128 * pair] = v.astype(jnp.bfloat16)

    scale = lax.rsqrt(jnp.sum(ssq[...], axis=1, keepdims=True) * (1.0 / D) + EPS)
    for i in range(TP):
        v = hall[i, 0:T, :].astype(jnp.float32) * scale
        hn[:, 256 * i : 256 * i + 256] = (v * gain_ref[i]).astype(jnp.bfloat16)
    v = hn[:, 2048:].astype(jnp.float32) * scale
    hn[:, 2048:] = (v * gain_last).astype(jnp.bfloat16)

    def project(lo, hi):
        total = None
        for i in range(TP):
            w = wall[F * i : F * i + 256, lo:hi]
            part = jnp.dot(hn[:, 256 * i : 256 * i + 256], w, preferred_element_type=jnp.float32)
            total = part if total is None else total + part
        for i in range(2):
            w = jnp.concatenate([wall[F * j + 256 : F * j + 320, lo:hi] for j in range(4 * i, 4 * i + 4)], axis=0)
            at = 2048 + 256 * i
            total = total + jnp.dot(hn[:, at : at + 256], w, preferred_element_type=jnp.float32)
        return total

    def norm_rotate(u, gain):
        mean = jnp.sum(u * u, axis=1, keepdims=True) * (1.0 / HD)
        u = u * lax.rsqrt(mean + EPS) * gain
        return u * cosr[...] + pltpu.roll(u, HD // 2, 1) * sinr[...]

    kvp = project(512, 768)
    keys = norm_rotate(kvp[:, 0:HD], kg_ref[...]).astype(jnp.bfloat16)
    vt = kvp[:, HD:].T.astype(jnp.bfloat16)
    for i in range(T // PAGE):
        kv[s * 8 + i] = keys[PAGE * i : PAGE * i + PAGE, :]
        kv[s * 8 + per + i] = vt[:, PAGE * i : PAGE * i + PAGE]
    kv_begin()

    for pair in range(G // 2):
        qp = project(256 * pair, 256 * pair + 256)
        for i in range(2):
            u = norm_rotate(qp[:, HD * i : HD * i + HD], qg_ref[...]).astype(jnp.bfloat16)
            qt[2 * pair + i] = u.astype(jnp.float32).T.astype(jnp.bfloat16)

    ones = jnp.where(lax.broadcasted_iota(jnp.int32, (VE - HD, T), 0) == 0, 1.0, 0.0).astype(jnp.bfloat16)

    def attend(rank, diagonal):
        keys = jnp.concatenate([kv[rank * 8 + i] for i in range(per)], axis=0)
        vals = jnp.concatenate([kv[rank * 8 + per + i] for i in range(per)], axis=1)
        vals = jnp.concatenate([vals, ones], axis=0)
        if not diagonal:
            key_slot = rank * T + lax.broadcasted_iota(jnp.int32, (T, HD), 0)
            member = (key_slot >= bounds[0:1, :]) & (key_slot < bounds[1:2, :])
            keys = jnp.concatenate([keys, jnp.where(member, 1.0, 0.0).astype(jnp.bfloat16)], axis=1)

        def score(h):
            if diagonal:
                return jnp.dot(keys, qt[h], preferred_element_type=jnp.float32)
            queries = jnp.concatenate([qt[h], other[...]], axis=0)
            return jnp.dot(keys, queries, preferred_element_type=jnp.float32)

        ahead = score(0)
        for h in range(G):
            scores = ahead
            if h + 1 < G:
                ahead = score(h + 1)
            if diagonal:
                key_slot = rank * T + lax.broadcasted_iota(jnp.int32, (T, T), 0)
                query_slot = rank * T + lax.broadcasted_iota(jnp.int32, (T, T), 1)
                allowed = (key_slot >= startr[0:1, :]) & (key_slot <= query_slot)
                scores = jnp.where(allowed, scores, EXCLUDED)
            top = jnp.max(scores, axis=0, keepdims=True)
            if not diagonal:
                old = mx[h]
                top = jnp.maximum(old, top)
            probs = jnp.exp2((scores - top) * SCALE).astype(jnp.bfloat16)
            sums = jnp.dot(vals, probs, preferred_element_type=jnp.float32)
            if diagonal:
                acc[h] = sums
            else:
                acc[h] = acc[h] * jnp.exp2((old - top) * SCALE) + sums
            mx[h] = top

    def attend_all(offsets):
        def one(k, carry):
            rank = seq_rank(*offsets[0])
            for i in range(1, len(offsets)):
                rank = jnp.where(k == i, seq_rank(*offsets[i]), rank)

            @pl.when((rank < s) & (rank + 8 >= s))
            def _():
                attend(rank, False)

            return carry

        lax.fori_loop(0, len(offsets), one, 0)

    attend(s, True)
    for name, piece in (("xm", 0), ("xp", 1), ("xm", 1), ("xp", 0), ("y", 0), ("y", 1)):
        kv_pass(name, piece)
    for name in ("y", "xm", "xp"):
        kv_share(name)
    gk.wait(seq_rank(0, 0, 1), None, 21)
    attend_all([(0, 0, 1), (0, 1, 0)])
    kv_pass("x2", 0)
    kv_pass("x2", 1)
    kv_share("x2")
    attend_all([(3, 0, 0), (1, 0, 0)])
    for name, piece in (("xmy", 0), ("xpy", 0), ("xmy", 1), ("xpy", 1)):
        kv_pass(name, piece)
    kv_share("xmy")
    kv_share("xpy")
    for name in ("y", "xm", "xp"):
        kv_sib(name)
    attend_all([(0, 1, 1), (3, 0, 1), (1, 0, 1), (3, 1, 0), (1, 1, 0)])
    kv_pass("x2y", 0)
    kv_pass("x2y", 1)
    kv_share("x2y")
    for name in ("x2", "xmy", "xpy"):
        kv_sib(name)
    attend_all([(2, 0, 0), (3, 1, 1), (1, 1, 1), (2, 0, 1), (2, 1, 0)])
    kv_sib("x2y")
    attend_all([(2, 1, 1)])

    for h in range(G):
        o = acc[h, 0:HD, :] / acc[h, HD : HD + 1, :]
        out_ref[:, HD * h : HD * h + HD] = o.T.astype(jnp.bfloat16)

    for i in range(per):
        kc_ref[i, 0] = kv[source[i]]
        page = kv[source[i] + per]
        vc_ref[i, 0] = page.astype(jnp.float32).T.astype(jnp.bfloat16)

    for copy in started:
        copy.wait_send()


def shards(hidden, norm_gain, query_weight, key_weight, value_weight, query_gain, key_gain, lengths, page_table):
    half = 1000000.0 ** -(np.arange(HD // 2, dtype=np.float32) * np.float32(2.0 / HD))
    freq = jnp.asarray(np.concatenate([half, half])[None, :].astype(np.float32))
    vmem = pl.BlockSpec(memory_space=pltpu.VMEM)
    smem = pl.BlockSpec(memory_space=pltpu.SMEM)
    return pl.pallas_call(
        kernel,
        out_shape=(
            jax.ShapeDtypeStruct((T, G * HD), jnp.bfloat16),
            jax.ShapeDtypeStruct((T // PAGE, 1, PAGE, HD), jnp.bfloat16),
            jax.ShapeDtypeStruct((T // PAGE, 1, PAGE, HD), jnp.bfloat16),
        ),
        in_specs=[vmem] * 8 + [smem] * 2,
        out_specs=(vmem,) * 3,
        scratch_shapes=[
            pltpu.VMEM((TP, HR, 256), jnp.bfloat16),
            pltpu.VMEM((D, NC), jnp.bfloat16),
            pltpu.VMEM((SEQ * 8, PAGE, HD), jnp.bfloat16),
            pltpu.VMEM((T, D), jnp.bfloat16),
            pltpu.VMEM((G, HD, T), jnp.bfloat16),
            pltpu.VMEM((G, VE, T), jnp.float32),
            pltpu.VMEM((G, 1, T), jnp.float32),
            pltpu.VMEM((T, HD), jnp.float32),
            pltpu.VMEM((T, HD), jnp.float32),
            pltpu.VMEM((8, T), jnp.int32),
            pltpu.VMEM((HD, T), jnp.bfloat16),
            pltpu.VMEM((8, HD), jnp.int32),
            pltpu.VMEM((T, HD), jnp.float32),
            pltpu.SemaphoreType.DMA((14,)),
            pltpu.SemaphoreType.DMA((14,)),
            pltpu.SemaphoreType.DMA((20,)),
            pltpu.SemaphoreType.DMA((20,)),
            pltpu.SemaphoreType.DMA((22,)),
            pltpu.SemaphoreType.DMA((22,)),
        ],
        compiler_params=pltpu.CompilerParams(
            collective_id=0, has_side_effects=True, vmem_limit_bytes=48 * 1024 * 1024
        ),
        cost_estimate=pl.CostEstimate(flops=7 * 10**9, bytes_accessed=4 * 10**6, transcendentals=10**7),
    )(
        hidden,
        norm_gain,
        query_weight,
        key_weight,
        value_weight,
        query_gain.reshape(1, HD),
        key_gain.reshape(1, HD),
        freq,
        lengths,
        page_table,
    )


def solution(mesh):
    return jax.shard_map(
        shards,
        mesh=mesh,
        in_specs=(
            P("seq", "tp"),
            P(),
            P("seq", "tp"),
            P("seq", "tp"),
            P("seq", "tp"),
            P(),
            P(),
            P(),
            P(),
        ),
        out_specs=(P("seq", "tp"), P("seq", "tp", None, None), P("seq", "tp", None, None)),
        check_vma=False,
    )
```

```python
import math

import jax
import jax.numpy as jnp
import numpy as np
from jax import lax
from jax.experimental import pallas as pl
from jax.experimental.pallas import tpu as pltpu
from jax.sharding import PartitionSpec as P

T = 512
F = 320
D = 2560
WR = 160
HD = 128
G = 4
NC = 768
PAGE = 128
PAGES = 64
NSEG = 8
SEQ = 16
TP = 8
EPS = 1e-6
EXCLUDED = -1e30
HR = 640
MESH = pl.DeviceIdType.MESH
SCALE = HD**-0.5 * math.log2(math.e)
VE = HD + 16


def kernel(
    hid_ref,
    gain_1d,
    wq_ref,
    wk_ref,
    wv_ref,
    qg_ref,
    kg_ref,
    freq_ref,
    len_ref,
    pt_ref,
    out_ref,
    kc_ref,
    vc_ref,
    hall,
    wall,
    kv,
    hn,
    qt,
    acc,
    mx,
    cosr,
    sinr,
    startr,
    other,
    bounds,
    ssq,
    hb,
    h_send,
    h_recv,
    w_send,
    w_recv,
    kv_send,
    kv_recv,
):
    s = lax.axis_index("seq")
    t = lax.axis_index("tp")
    yh, x, c = s // 8, (s // 2) % 4, s % 2
    yl, z = t // 4, t % 4

    def seq_rank(dx, dy, dc):
        return ((yh + dy) % 2) * 8 + ((x + dx) % 4) * 2 + (c + dc) % 2

    def tp_rank(dz, dy):
        return ((yl + dy) % 2) * 4 + (z + dz) % 4

    sib = {"seq": seq_rank(0, 0, 1), "tp": t}
    xp = {"seq": seq_rank(1, 0, 0), "tp": t}
    xm = {"seq": seq_rank(3, 0, 0), "tp": t}
    yhp = {"seq": seq_rank(0, 1, 0), "tp": t}
    zp = {"seq": s, "tp": tp_rank(1, 0)}
    zm = {"seq": s, "tp": tp_rank(3, 0)}
    ylp = {"seq": s, "tp": tp_rank(0, 1)}
    barrier = pltpu.get_barrier_semaphore()
    for peer in (sib, xp, xm, yhp, zp, zm, ylp):
        pl.semaphore_signal(barrier, inc=1, device_id=peer, device_id_type=MESH)

    hall[t, 0:T, :] = hid_ref[:, 0:256]
    for q in range(4):
        hall[t, T : T + 128, 64 * q : 64 * q + 64] = hid_ref[128 * q : 128 * q + 128, 256:320]
    own_w = pl.ds(pl.multiple_of(s * WR, 16), WR)
    wall[own_w, 0:512] = wq_ref[...].astype(jnp.bfloat16)
    wall[own_w, 512:640] = wk_ref[...].astype(jnp.bfloat16)
    wall[own_w, 640:768] = wv_ref[...].astype(jnp.bfloat16)

    pl.semaphore_wait(barrier, 7)

    started = []

    class Gather:
        def __init__(self, region, send, recv):
            self.region, self.send, self.recv, self.sends = region, send, recv, 0

        def go(self, rank, half, role, peer):
            ref = self.region(rank, half)
            copy = pltpu.make_async_remote_copy(
                src_ref=ref,
                dst_ref=ref,
                send_sem=self.send.at[self.sends],
                recv_sem=self.recv.at[role],
                device_id=peer,
                device_id_type=MESH,
            )
            self.sends += 1
            copy.start()
            started.append(copy)

        def wait(self, rank, half, role):
            ref = self.region(rank, half)
            pltpu.make_async_remote_copy(
                src_ref=ref,
                dst_ref=ref,
                send_sem=self.send.at[0],
                recv_sem=self.recv.at[role],
                device_id=sib,
                device_id_type=MESH,
            ).wait_recv()

    def h_region(rank, half):
        if half is None:
            return hall.at[rank]
        return hall.at[rank, pl.ds(half * (HR // 2), HR // 2), :]

    def w_region(rank, half):
        if half is None:
            return wall.at[pl.ds(pl.multiple_of(rank * WR, 16), WR), :]
        return wall.at[pl.ds(pl.multiple_of(rank * WR + half * (WR // 2), 16), WR // 2), :]

    def kv_region(rank, half):
        if half is None:
            return kv.at[pl.ds(rank * 8, 8)]
        return kv.at[pl.ds(rank * 8 + half * 4, 4)]

    seq_roles = [(0, 1, None), (3, 0, None), (3, 1, None), (1, 0, None), (1, 1, None), (2, 0, 0), (2, 1, 0), (2, 0, 1), (2, 1, 1)]
    seq_forward = {
        0: ((None, 2, xp), (None, 4, xm)),
        1: ((0, 5, xp),),
        2: ((0, 6, xp),),
        3: ((1, 7, xm),),
        4: ((1, 8, xm),),
    }

    def seq_pass(g, role):
        dx, dy, half = seq_roles[role]
        rank = seq_rank(dx, dy, 0)
        g.wait(rank, half, role)
        for part, to, peer in seq_forward.get(role, ()):
            g.go(rank, part, to, peer)
        g.go(rank, half, 11 + role, sib)

    def seq_sib(g, role):
        if role is None:
            g.wait(seq_rank(0, 0, 1), None, 10)
        else:
            dx, dy, half = seq_roles[role]
            g.wait(seq_rank(dx, dy, 1), half, 11 + role)

    tp_roles = {"zm": (3, 0), "zp": (1, 0), "y": (0, 1), "z2": (2, 0), "zmy": (3, 1), "zpy": (1, 1), "z2y": (2, 1)}
    tp_index = {name: 2 * i for i, name in enumerate(tp_roles)}
    tp_forward = {
        ("zm", 0): (("z2", zp),),
        ("zp", 1): (("z2", zm),),
        ("y", 0): (("zmy", zp), ("zpy", zm)),
        ("y", 1): (("zmy", zp), ("zpy", zm)),
        ("z2", 0): (("z2y", ylp),),
        ("z2", 1): (("z2y", ylp),),
    }

    def tp_pass(name, piece):
        rank = tp_rank(*tp_roles[name])
        gh.wait(rank, piece, tp_index[name] + piece)
        for to, peer in tp_forward.get((name, piece), ()):
            gh.go(rank, piece, tp_index[to] + piece, peer)

    def tp_begin(name, piece, peer):
        gh.go(t, piece, tp_index[name] + piece, peer)

    kv_roles = {"xm": (3, 0), "xp": (1, 0), "y": (0, 1), "x2": (2, 0), "xmy": (3, 1), "xpy": (1, 1), "x2y": (2, 1)}
    kv_index = {name: i for i, name in enumerate(kv_roles)}
    kv_forward = {
        ("xm", 0): (("x2", xp),),
        ("xp", 1): (("x2", xm),),
        ("y", 0): (("xmy", xp), ("xpy", xm)),
        ("y", 1): (("xmy", xp), ("xpy", xm)),
        ("x2", 0): (("x2y", yhp),),
        ("x2", 1): (("x2y", yhp),),
    }

    def kv_begin():
        for name, piece, peer in (("xm", 0, xp), ("xp", 1, xm), ("y", 0, yhp), ("y", 1, yhp), ("xm", 1, xp), ("xp", 0, xm)):
            gk.go(s, piece, 2 * kv_index[name] + piece, peer)
        gk.go(s, None, 21, sib)

    def kv_pass(name, piece):
        rank = seq_rank(*kv_roles[name], 0)
        gk.wait(rank, piece, 2 * kv_index[name] + piece)
        for to, peer in kv_forward.get((name, piece), ()):
            gk.go(rank, piece, 2 * kv_index[to] + piece, peer)

    def kv_share(name):
        gk.go(seq_rank(*kv_roles[name], 0), None, 14 + kv_index[name], sib)

    def kv_sib(name):
        gk.wait(seq_rank(*kv_roles[name], 1), None, 14 + kv_index[name])

    gh = Gather(h_region, h_send, h_recv)
    gw = Gather(w_region, w_send, w_recv)
    gk = Gather(kv_region, kv_send, kv_recv)

    gw.go(s, None, 0, yhp)
    tp_begin("y", 0, ylp)
    tp_begin("y", 1, ylp)
    gw.go(s, None, 1, xp)
    gw.go(s, None, 3, xm)
    tp_begin("zm", 0, zp)
    tp_begin("zp", 1, zm)
    tp_begin("zm", 1, zp)
    tp_begin("zp", 0, zm)
    gw.go(s, None, 10, sib)

    def start_of(slots):
        start = jnp.zeros_like(slots)
        end = jnp.int32(0)
        for i in range(NSEG):
            end = end + len_ref[i]
            start = jnp.where(slots >= end, end, start)
        return start

    rows = s * T + lax.broadcasted_iota(jnp.int32, (T, HD), 0)
    position = (rows - start_of(rows)).astype(jnp.float32)
    angles = position * freq_ref[...]
    cosr[...] = jnp.cos(angles)
    lane = lax.broadcasted_iota(jnp.int32, (T, HD), 1)
    sine = jnp.sin(angles)
    sinr[...] = jnp.where(lane < HD // 2, -sine, sine)
    slots = s * T + lax.broadcasted_iota(jnp.int32, (8, T), 1)
    startr[...] = start_of(slots)
    label = lax.broadcasted_iota(jnp.int32, (HD, T), 0)
    lane_label = lax.broadcasted_iota(jnp.int32, (8, HD), 1)
    query_slot = s * T + lax.broadcasted_iota(jnp.int32, (HD, T), 1)
    mine = label >= NSEG
    low = jnp.zeros((8, HD), jnp.int32)
    high = jnp.zeros((8, HD), jnp.int32)
    end = jnp.int32(0)
    for i in range(NSEG):
        begin, end = end, end + len_ref[i]
        mine = mine | ((label == i) & (query_slot >= begin) & (query_slot < end))
        low = jnp.where(lane_label == i, begin, low)
        high = jnp.where(lane_label == i, end, high)
    other[...] = jnp.where(mine, 0.0, EXCLUDED).astype(jnp.bfloat16)
    bounds[0:1, :] = low[0:1, :]
    bounds[1:2, :] = high[0:1, :]

    per = T // PAGE
    source = [jnp.int32(0)] * per
    for b in range(PAGES):
        page = pt_ref[b] - s * per
        row = (b // per) * 2 * per + b % per
        source = [jnp.where(page == i, row, f) for i, f in enumerate(source)]

    ssq[...] = jnp.zeros_like(ssq)

    def add_squares(rank):
        v = hall[rank, 0:T, :].astype(jnp.float32)
        v = v * v
        ssq[...] += v[:, 0:HD] + v[:, HD:]

    add_squares(t)
    seq_pass(gw, 1)
    seq_pass(gw, 3)
    for name, piece in (("zm", 0), ("zp", 0), ("zp", 1), ("zm", 1)):
        tp_pass(name, piece)
    seq_pass(gw, 0)
    tp_pass("y", 0)
    tp_pass("y", 1)
    seq_pass(gw, 5)
    tp_pass("z2", 0)
    seq_pass(gw, 7)
    tp_pass("z2", 1)
    seq_pass(gw, 2)
    seq_pass(gw, 4)
    for dz, dy in ((0, 1), (1, 0), (3, 0), (2, 0)):
        add_squares(tp_rank(dz, dy))
    for name, piece in (("zmy", 0), ("zpy", 0), ("zmy", 1), ("zpy", 1)):
        tp_pass(name, piece)
    seq_pass(gw, 6)
    seq_pass(gw, 8)
    add_squares(tp_rank(3, 1))
    add_squares(tp_rank(1, 1))
    half_lane = lax.broadcasted_iota(jnp.int32, (128, 128), 1) < 64

    def unpack(pair):
        for col in range(2):
            lanes = slice(128 * col, 128 * col + 128)
            a = hall[2 * pair, T : T + 128, lanes].astype(jnp.float32)
            b = hall[2 * pair + 1, T : T + 128, lanes].astype(jnp.float32)
            low = jnp.where(half_lane, a, pltpu.roll(b, 64, 1))
            high = jnp.where(half_lane, pltpu.roll(a, 64, 1), b)
            for q, v in ((2 * col, low), (2 * col + 1, high)):
                where = slice(128 * q, 128 * q + 128)
                ssq[where, :] += v * v
                hb[pair, where, :] = v.astype(jnp.bfloat16)

    corner = tp_rank(2, 1)
    for i in range(1, TP // 2):
        unpack((corner // 2 + i) % (TP // 2))
    gain_row = gain_1d[...].reshape(1, D)
    gain_ref = [gain_row[:, F * i : F * i + 256] for i in range(TP)]
    gain_last = jnp.concatenate([gain_row[:, F * i + 256 : F * i + F] for i in range(TP)], axis=1)
    seq_sib(gw, None)
    for role in range(9):
        seq_sib(gw, role)
    tp_pass("z2y", 0)
    tp_pass("z2y", 1)
    add_squares(corner)
    unpack(corner // 2)

    scale = lax.rsqrt(jnp.sum(ssq[...], axis=1, keepdims=True) * (1.0 / D) + EPS)
    for i in range(TP):
        v = hall[i, 0:T, :].astype(jnp.float32) * scale
        hn[:, 256 * i : 256 * i + 256] = (v * gain_ref[i]).astype(jnp.bfloat16)
    for i in range(TP // 2):
        v = hb[i].astype(jnp.float32) * scale
        at = 2048 + HD * i
        hn[:, at : at + HD] = (v * gain_last[:, HD * i : HD * i + HD]).astype(jnp.bfloat16)

    def project(lo, hi):
        total = None
        for i in range(TP):
            w = wall[F * i : F * i + 256, lo:hi]
            part = jnp.dot(hn[:, 256 * i : 256 * i + 256], w, preferred_element_type=jnp.float32)
            total = part if total is None else total + part
        for i in range(2):
            w = jnp.concatenate([wall[F * j + 256 : F * j + 320, lo:hi] for j in range(4 * i, 4 * i + 4)], axis=0)
            at = 2048 + 256 * i
            total = total + jnp.dot(hn[:, at : at + 256], w, preferred_element_type=jnp.float32)
        return total

    def norm_rotate(u, gain):
        mean = jnp.sum(u * u, axis=1, keepdims=True) * (1.0 / HD)
        u = u * lax.rsqrt(mean + EPS) * gain
        return u * cosr[...] + pltpu.roll(u, HD // 2, 1) * sinr[...]

    kvp = project(512, 768)
    keys = norm_rotate(kvp[:, 0:HD], kg_ref[...]).astype(jnp.bfloat16)
    vt = kvp[:, HD:].T.astype(jnp.bfloat16)
    for i in range(T // PAGE):
        kv[s * 8 + i] = keys[PAGE * i : PAGE * i + PAGE, :]
        kv[s * 8 + per + i] = vt[:, PAGE * i : PAGE * i + PAGE]
    kv_begin()

    for pair in range(G // 2):
        qp = project(256 * pair, 256 * pair + 256)
        for i in range(2):
            u = norm_rotate(qp[:, HD * i : HD * i + HD], qg_ref[...]).astype(jnp.bfloat16)
            qt[2 * pair + i] = u.astype(jnp.float32).T.astype(jnp.bfloat16)

    ones = jnp.where(lax.broadcasted_iota(jnp.int32, (VE - HD, T), 0) == 0, 1.0, 0.0).astype(jnp.bfloat16)

    def blocks(rank):
        keys = jnp.concatenate([kv[rank * 8 + i] for i in range(per)], axis=0)
        vals = jnp.concatenate([kv[rank * 8 + per + i] for i in range(per)], axis=1)
        return keys, jnp.concatenate([vals, ones], axis=0)

    def attend_own():
        keys, vals = blocks(s)
        wide = T // 2
        parts = [(h, half) for h in range(G) for half in range(2)]

        def score(h, half):
            queries = qt[h][:, wide * half : wide * half + wide]
            return jnp.dot(keys[: wide * (half + 1), :], queries, preferred_element_type=jnp.float32)

        ahead = score(*parts[0])
        for i, (h, half) in enumerate(parts):
            scores, count, at = ahead, wide * (half + 1), slice(wide * half, wide * half + wide)
            if i + 1 < len(parts):
                ahead = score(*parts[i + 1])
            key_slot = lax.broadcasted_iota(jnp.int32, (count, wide), 0)
            query_slot = wide * half + lax.broadcasted_iota(jnp.int32, (count, wide), 1)
            allowed = (key_slot >= startr[0:1, at] - s * T) & (key_slot <= query_slot)
            scores = jnp.where(allowed, scores, EXCLUDED)
            top = jnp.max(scores, axis=0, keepdims=True)
            probs = jnp.exp2((scores - top) * SCALE).astype(jnp.bfloat16)
            acc[h, :, at] = jnp.dot(vals[:, :count], probs, preferred_element_type=jnp.float32)
            mx[h, :, at] = top

    def attend(rank):
        keys, vals = blocks(rank)
        key_slot = rank * T + lax.broadcasted_iota(jnp.int32, (T, HD), 0)
        member = (key_slot >= bounds[0:1, :]) & (key_slot < bounds[1:2, :])
        keys = jnp.concatenate([keys, jnp.where(member, 1.0, 0.0).astype(jnp.bfloat16)], axis=1)

        def score(h):
            queries = jnp.concatenate([qt[h], other[...]], axis=0)
            return jnp.dot(keys, queries, preferred_element_type=jnp.float32)

        ahead = score(0)
        for h in range(G):
            scores = ahead
            if h + 1 < G:
                ahead = score(h + 1)
            old = mx[h]
            top = jnp.maximum(old, jnp.max(scores, axis=0, keepdims=True))
            probs = jnp.exp2((scores - top) * SCALE).astype(jnp.bfloat16)
            sums = jnp.dot(vals, probs, preferred_element_type=jnp.float32)
            acc[h] = acc[h] * jnp.exp2((old - top) * SCALE) + sums
            mx[h] = top

    def attend_all(offsets):
        def one(k, carry):
            rank = seq_rank(*offsets[0])
            for i in range(1, len(offsets)):
                rank = jnp.where(k == i, seq_rank(*offsets[i]), rank)

            @pl.when((rank < s) & (rank + 8 >= s))
            def _():
                attend(rank)

            return carry

        lax.fori_loop(0, len(offsets), one, 0)

    attend_own()
    for name, piece in (("xm", 0), ("xp", 1), ("xm", 1), ("xp", 0), ("y", 0), ("y", 1)):
        kv_pass(name, piece)
    for name in ("y", "xm", "xp"):
        kv_share(name)
    gk.wait(seq_rank(0, 0, 1), None, 21)
    attend_all([(0, 0, 1), (0, 1, 0)])
    kv_pass("x2", 0)
    kv_pass("x2", 1)
    kv_share("x2")
    attend_all([(3, 0, 0), (1, 0, 0)])
    for name, piece in (("xmy", 0), ("xpy", 0), ("xmy", 1), ("xpy", 1)):
        kv_pass(name, piece)
    kv_share("xmy")
    kv_share("xpy")
    for name in ("y", "xm", "xp"):
        kv_sib(name)
    attend_all([(0, 1, 1), (3, 0, 1), (1, 0, 1), (3, 1, 0), (1, 1, 0)])
    kv_pass("x2y", 0)
    kv_pass("x2y", 1)
    kv_share("x2y")
    for name in ("x2", "xmy", "xpy"):
        kv_sib(name)
    attend_all([(2, 0, 0), (3, 1, 1), (1, 1, 1), (2, 0, 1), (2, 1, 0)])
    kv_sib("x2y")
    attend_all([(2, 1, 1)])

    for h in range(G):
        o = acc[h, 0:HD, :] * (1.0 / acc[h, HD : HD + 1, :])
        out_ref[:, HD * h : HD * h + HD] = o.T.astype(jnp.bfloat16)

    for i in range(per):
        kc_ref[i, 0] = kv[source[i]]
        page = kv[source[i] + per]
        vc_ref[i, 0] = page.astype(jnp.float32).T.astype(jnp.bfloat16)

    for copy in started:
        copy.wait_send()


def shards(hidden, norm_gain, query_weight, key_weight, value_weight, query_gain, key_gain, lengths, page_table):
    half = 1000000.0 ** -(np.arange(HD // 2, dtype=np.float32) * np.float32(2.0 / HD))
    freq = jnp.asarray(np.concatenate([half, half])[None, :].astype(np.float32))
    vmem = pl.BlockSpec(memory_space=pltpu.VMEM)
    smem = pl.BlockSpec(memory_space=pltpu.SMEM)
    return pl.pallas_call(
        kernel,
        out_shape=(
            jax.ShapeDtypeStruct((T, G * HD), jnp.bfloat16),
            jax.ShapeDtypeStruct((T // PAGE, 1, PAGE, HD), jnp.bfloat16),
            jax.ShapeDtypeStruct((T // PAGE, 1, PAGE, HD), jnp.bfloat16),
        ),
        in_specs=[vmem] * 8 + [smem] * 2,
        out_specs=(vmem,) * 3,
        scratch_shapes=[
            pltpu.VMEM((TP, HR, 256), jnp.bfloat16),
            pltpu.VMEM((D, NC), jnp.bfloat16),
            pltpu.VMEM((SEQ * 8, PAGE, HD), jnp.bfloat16),
            pltpu.VMEM((T, D), jnp.bfloat16),
            pltpu.VMEM((G, HD, T), jnp.bfloat16),
            pltpu.VMEM((G, VE, T), jnp.float32),
            pltpu.VMEM((G, 1, T), jnp.float32),
            pltpu.VMEM((T, HD), jnp.float32),
            pltpu.VMEM((T, HD), jnp.float32),
            pltpu.VMEM((8, T), jnp.int32),
            pltpu.VMEM((HD, T), jnp.bfloat16),
            pltpu.VMEM((8, HD), jnp.int32),
            pltpu.VMEM((T, HD), jnp.float32),
            pltpu.VMEM((TP // 2, T, HD), jnp.bfloat16),
            pltpu.SemaphoreType.DMA((14,)),
            pltpu.SemaphoreType.DMA((14,)),
            pltpu.SemaphoreType.DMA((20,)),
            pltpu.SemaphoreType.DMA((20,)),
            pltpu.SemaphoreType.DMA((22,)),
            pltpu.SemaphoreType.DMA((22,)),
        ],
        compiler_params=pltpu.CompilerParams(
            collective_id=0, has_side_effects=True, vmem_limit_bytes=48 * 1024 * 1024
        ),
        cost_estimate=pl.CostEstimate(flops=7 * 10**9, bytes_accessed=4 * 10**6, transcendentals=10**7),
    )(
        hidden,
        norm_gain,
        query_weight,
        key_weight,
        value_weight,
        query_gain.reshape(1, HD),
        key_gain.reshape(1, HD),
        freq,
        lengths,
        page_table,
    )


def solution(mesh):
    return jax.shard_map(
        shards,
        mesh=mesh,
        in_specs=(
            P("seq", "tp"),
            P(),
            P("seq", "tp"),
            P("seq", "tp"),
            P("seq", "tp"),
            P(),
            P(),
            P(),
            P(),
        ),
        out_specs=(P("seq", "tp"), P("seq", "tp", None, None), P("seq", "tp", None, None)),
        check_vma=False,
    )
```

```python
import math

import jax
import jax.numpy as jnp
import numpy as np
from jax import lax
from jax.experimental import pallas as pl
from jax.experimental.pallas import tpu as pltpu
from jax.sharding import PartitionSpec as P

T = 512
F = 320
D = 2560
WR = 160
HD = 128
G = 4
NC = 768
PAGE = 128
PAGES = 64
NSEG = 8
SEQ = 16
TP = 8
EPS = 1e-6
EXCLUDED = -1e30
HR = 640
MESH = pl.DeviceIdType.MESH
SCALE = HD**-0.5 * math.log2(math.e)
VE = HD + 16


def kernel(
    hid_ref,
    gain_1d,
    wq_ref,
    wk_ref,
    wv_ref,
    qg_ref,
    kg_ref,
    freq_ref,
    len_ref,
    pt_ref,
    out_ref,
    kc_ref,
    vc_ref,
    hall,
    wall,
    kv,
    hn,
    qt,
    acc,
    mx,
    cosr,
    sinr,
    startr,
    other,
    bounds,
    ssq,
    hb,
    h_send,
    h_recv,
    w_send,
    w_recv,
    kv_send,
    kv_recv,
):
    s = lax.axis_index("seq")
    t = lax.axis_index("tp")
    yh, x, c = s // 8, (s // 2) % 4, s % 2
    yl, z = t // 4, t % 4

    def seq_rank(dx, dy, dc):
        return ((yh + dy) % 2) * 8 + ((x + dx) % 4) * 2 + (c + dc) % 2

    def tp_rank(dz, dy):
        return ((yl + dy) % 2) * 4 + (z + dz) % 4

    sib = {"seq": seq_rank(0, 0, 1), "tp": t}
    xp = {"seq": seq_rank(1, 0, 0), "tp": t}
    xm = {"seq": seq_rank(3, 0, 0), "tp": t}
    yhp = {"seq": seq_rank(0, 1, 0), "tp": t}
    zp = {"seq": s, "tp": tp_rank(1, 0)}
    zm = {"seq": s, "tp": tp_rank(3, 0)}
    ylp = {"seq": s, "tp": tp_rank(0, 1)}
    barrier = pltpu.get_barrier_semaphore()
    for peer in (sib, xp, xm, yhp, zp, zm, ylp):
        pl.semaphore_signal(barrier, inc=1, device_id=peer, device_id_type=MESH)

    hall[t, 0:T, :] = hid_ref[:, 0:256]
    for q in range(4):
        hall[t, T : T + 128, 64 * q : 64 * q + 64] = hid_ref[128 * q : 128 * q + 128, 256:320]
    own_w = pl.ds(pl.multiple_of(s * WR, 16), WR)
    wall[own_w, 0:512] = wq_ref[...].astype(jnp.bfloat16)
    wall[own_w, 512:640] = wk_ref[...].astype(jnp.bfloat16)
    wall[own_w, 640:768] = wv_ref[...].astype(jnp.bfloat16)

    pl.semaphore_wait(barrier, 7)

    started = []

    class Gather:
        def __init__(self, region, send, recv):
            self.region, self.send, self.recv, self.sends = region, send, recv, 0

        def go(self, rank, half, role, peer):
            ref = self.region(rank, half)
            copy = pltpu.make_async_remote_copy(
                src_ref=ref,
                dst_ref=ref,
                send_sem=self.send.at[self.sends],
                recv_sem=self.recv.at[role],
                device_id=peer,
                device_id_type=MESH,
            )
            self.sends += 1
            copy.start()
            started.append(copy)

        def wait(self, rank, half, role):
            ref = self.region(rank, half)
            pltpu.make_async_remote_copy(
                src_ref=ref,
                dst_ref=ref,
                send_sem=self.send.at[0],
                recv_sem=self.recv.at[role],
                device_id=sib,
                device_id_type=MESH,
            ).wait_recv()

    def h_region(rank, half):
        if half is None:
            return hall.at[rank]
        return hall.at[rank, pl.ds(half * (HR // 2), HR // 2), :]

    def w_region(rank, half):
        if half is None:
            return wall.at[pl.ds(pl.multiple_of(rank * WR, 16), WR), :]
        return wall.at[pl.ds(pl.multiple_of(rank * WR + half * (WR // 2), 16), WR // 2), :]

    def kv_region(rank, half):
        if half is None:
            return kv.at[pl.ds(rank * 8, 8)]
        return kv.at[pl.ds(rank * 8 + half * 4, 4)]

    seq_roles = [(0, 1, None), (3, 0, None), (3, 1, None), (1, 0, None), (1, 1, None), (2, 0, 0), (2, 1, 0), (2, 0, 1), (2, 1, 1)]
    seq_forward = {
        0: ((None, 2, xp), (None, 4, xm)),
        1: ((0, 5, xp),),
        2: ((0, 6, xp),),
        3: ((1, 7, xm),),
        4: ((1, 8, xm),),
    }

    def seq_pass(g, role):
        dx, dy, half = seq_roles[role]
        rank = seq_rank(dx, dy, 0)
        g.wait(rank, half, role)
        for part, to, peer in seq_forward.get(role, ()):
            g.go(rank, part, to, peer)
        g.go(rank, half, 11 + role, sib)

    def seq_sib(g, role):
        if role is None:
            g.wait(seq_rank(0, 0, 1), None, 10)
        else:
            dx, dy, half = seq_roles[role]
            g.wait(seq_rank(dx, dy, 1), half, 11 + role)

    tp_roles = {"zm": (3, 0), "zp": (1, 0), "y": (0, 1), "z2": (2, 0), "zmy": (3, 1), "zpy": (1, 1), "z2y": (2, 1)}
    tp_index = {name: 2 * i for i, name in enumerate(tp_roles)}
    tp_forward = {
        ("zm", 0): (("z2", zp),),
        ("zp", 1): (("z2", zm),),
        ("y", 0): (("zmy", zp), ("zpy", zm)),
        ("y", 1): (("zmy", zp), ("zpy", zm)),
        ("z2", 0): (("z2y", ylp),),
        ("z2", 1): (("z2y", ylp),),
    }

    def tp_pass(name, piece):
        rank = tp_rank(*tp_roles[name])
        gh.wait(rank, piece, tp_index[name] + piece)
        for to, peer in tp_forward.get((name, piece), ()):
            gh.go(rank, piece, tp_index[to] + piece, peer)

    def tp_begin(name, piece, peer):
        gh.go(t, piece, tp_index[name] + piece, peer)

    kv_roles = {"xm": (3, 0), "xp": (1, 0), "y": (0, 1), "x2": (2, 0), "xmy": (3, 1), "xpy": (1, 1), "x2y": (2, 1)}
    kv_index = {name: i for i, name in enumerate(kv_roles)}
    kv_forward = {
        ("xm", 0): (("x2", xp),),
        ("xp", 1): (("x2", xm),),
        ("y", 0): (("xmy", xp), ("xpy", xm)),
        ("y", 1): (("xmy", xp), ("xpy", xm)),
        ("x2", 0): (("x2y", yhp),),
        ("x2", 1): (("x2y", yhp),),
    }

    def kv_begin():
        for name, piece, peer in (("y", 0, yhp), ("y", 1, yhp), ("xm", 0, xp), ("xp", 1, xm), ("xm", 1, xp), ("xp", 0, xm)):
            gk.go(s, piece, 2 * kv_index[name] + piece, peer)
        gk.go(s, None, 21, sib)

    def kv_pass(name, piece):
        rank = seq_rank(*kv_roles[name], 0)
        gk.wait(rank, piece, 2 * kv_index[name] + piece)
        for to, peer in kv_forward.get((name, piece), ()):
            gk.go(rank, piece, 2 * kv_index[to] + piece, peer)

    def kv_share(name):
        gk.go(seq_rank(*kv_roles[name], 0), None, 14 + kv_index[name], sib)

    def kv_sib(name):
        gk.wait(seq_rank(*kv_roles[name], 1), None, 14 + kv_index[name])

    gh = Gather(h_region, h_send, h_recv)
    gw = Gather(w_region, w_send, w_recv)
    gk = Gather(kv_region, kv_send, kv_recv)

    gw.go(s, None, 0, yhp)
    tp_begin("y", 0, ylp)
    tp_begin("y", 1, ylp)
    gw.go(s, None, 1, xp)
    gw.go(s, None, 3, xm)
    tp_begin("zm", 0, zp)
    tp_begin("zp", 1, zm)
    tp_begin("zm", 1, zp)
    tp_begin("zp", 0, zm)
    gw.go(s, None, 10, sib)

    def start_of(slots):
        start = jnp.zeros_like(slots)
        end = jnp.int32(0)
        for i in range(NSEG):
            end = end + len_ref[i]
            start = jnp.where(slots >= end, end, start)
        return start

    rows = s * T + lax.broadcasted_iota(jnp.int32, (T, HD), 0)
    position = (rows - start_of(rows)).astype(jnp.float32)
    angles = position * freq_ref[...]
    cosr[...] = jnp.cos(angles)
    lane = lax.broadcasted_iota(jnp.int32, (T, HD), 1)
    sine = jnp.sin(angles)
    sinr[...] = jnp.where(lane < HD // 2, -sine, sine)
    slots = s * T + lax.broadcasted_iota(jnp.int32, (8, T), 1)
    startr[...] = start_of(slots)
    label = lax.broadcasted_iota(jnp.int32, (HD, T), 0)
    lane_label = lax.broadcasted_iota(jnp.int32, (8, HD), 1)
    query_slot = s * T + lax.broadcasted_iota(jnp.int32, (HD, T), 1)
    mine = label >= NSEG
    low = jnp.zeros((8, HD), jnp.int32)
    high = jnp.zeros((8, HD), jnp.int32)
    end = jnp.int32(0)
    for i in range(NSEG):
        begin, end = end, end + len_ref[i]
        mine = mine | ((label == i) & (query_slot >= begin) & (query_slot < end))
        low = jnp.where(lane_label == i, begin, low)
        high = jnp.where(lane_label == i, end, high)
    other[...] = jnp.where(mine, 0.0, EXCLUDED).astype(jnp.bfloat16)
    bounds[0:1, :] = low[0:1, :]
    bounds[1:2, :] = high[0:1, :]

    per = T // PAGE
    source = [jnp.int32(0)] * per
    for b in range(PAGES):
        page = pt_ref[b] - s * per
        row = (b // per) * 2 * per + b % per
        source = [jnp.where(page == i, row, f) for i, f in enumerate(source)]

    ssq[...] = jnp.zeros_like(ssq)

    def add_squares(rank):
        v = hall[rank, 0:T, :].astype(jnp.float32)
        v = v * v
        ssq[...] += v[:, 0:HD] + v[:, HD:]

    add_squares(t)
    seq_pass(gw, 1)
    seq_pass(gw, 3)
    for name, piece in (("zm", 0), ("zp", 0), ("zp", 1), ("zm", 1)):
        tp_pass(name, piece)
    seq_pass(gw, 0)
    tp_pass("y", 0)
    tp_pass("y", 1)
    seq_pass(gw, 5)
    tp_pass("z2", 0)
    seq_pass(gw, 7)
    tp_pass("z2", 1)
    seq_pass(gw, 2)
    seq_pass(gw, 4)
    for dz, dy in ((0, 1), (1, 0), (3, 0), (2, 0)):
        add_squares(tp_rank(dz, dy))
    for name, piece in (("zmy", 0), ("zpy", 0), ("zmy", 1), ("zpy", 1)):
        tp_pass(name, piece)
    seq_pass(gw, 6)
    seq_pass(gw, 8)
    add_squares(tp_rank(3, 1))
    add_squares(tp_rank(1, 1))
    half_lane = lax.broadcasted_iota(jnp.int32, (128, 128), 1) < 64

    def unpack(pair):
        for col in range(2):
            lanes = slice(128 * col, 128 * col + 128)
            a = hall[2 * pair, T : T + 128, lanes].astype(jnp.float32)
            b = hall[2 * pair + 1, T : T + 128, lanes].astype(jnp.float32)
            low = jnp.where(half_lane, a, pltpu.roll(b, 64, 1))
            high = jnp.where(half_lane, pltpu.roll(a, 64, 1), b)
            for q, v in ((2 * col, low), (2 * col + 1, high)):
                where = slice(128 * q, 128 * q + 128)
                ssq[where, :] += v * v
                hb[pair, where, :] = v.astype(jnp.bfloat16)

    corner = tp_rank(2, 1)
    for i in range(1, TP // 2):
        unpack((corner // 2 + i) % (TP // 2))
    gain_row = gain_1d[...].reshape(1, D)
    gain_ref = [gain_row[:, F * i : F * i + 256] for i in range(TP)]
    gain_last = jnp.concatenate([gain_row[:, F * i + 256 : F * i + F] for i in range(TP)], axis=1)
    seq_sib(gw, None)
    for role in range(9):
        seq_sib(gw, role)
    tp_pass("z2y", 0)
    tp_pass("z2y", 1)
    add_squares(corner)
    unpack(corner // 2)

    scale = lax.rsqrt(jnp.sum(ssq[...], axis=1, keepdims=True) * (1.0 / D) + EPS)
    for i in range(TP):
        v = hall[i, 0:T, :].astype(jnp.float32) * scale
        hn[:, 256 * i : 256 * i + 256] = (v * gain_ref[i]).astype(jnp.bfloat16)
    for i in range(TP // 2):
        v = hb[i].astype(jnp.float32) * scale
        at = 2048 + HD * i
        hn[:, at : at + HD] = (v * gain_last[:, HD * i : HD * i + HD]).astype(jnp.bfloat16)

    def project(lo, hi):
        total = None
        for i in range(TP):
            w = wall[F * i : F * i + 256, lo:hi]
            part = jnp.dot(hn[:, 256 * i : 256 * i + 256], w, preferred_element_type=jnp.float32)
            total = part if total is None else total + part
        for i in range(2):
            w = jnp.concatenate([wall[F * j + 256 : F * j + 320, lo:hi] for j in range(4 * i, 4 * i + 4)], axis=0)
            at = 2048 + 256 * i
            total = total + jnp.dot(hn[:, at : at + 256], w, preferred_element_type=jnp.float32)
        return total

    def norm_rotate(u, gain):
        mean = jnp.sum(u * u, axis=1, keepdims=True) * (1.0 / HD)
        u = u * lax.rsqrt(mean + EPS) * gain
        return u * cosr[...] + pltpu.roll(u, HD // 2, 1) * sinr[...]

    kvp = project(512, 768)
    keys = norm_rotate(kvp[:, 0:HD], kg_ref[...]).astype(jnp.bfloat16)
    vt = kvp[:, HD:].T.astype(jnp.bfloat16)
    for i in range(T // PAGE):
        kv[s * 8 + i] = keys[PAGE * i : PAGE * i + PAGE, :]
        kv[s * 8 + per + i] = vt[:, PAGE * i : PAGE * i + PAGE]
    kv_begin()

    for pair in range(G // 2):
        qp = project(256 * pair, 256 * pair + 256)
        for i in range(2):
            u = norm_rotate(qp[:, HD * i : HD * i + HD], qg_ref[...]).astype(jnp.bfloat16)
            qt[2 * pair + i] = u.astype(jnp.float32).T.astype(jnp.bfloat16)

    ones = jnp.where(lax.broadcasted_iota(jnp.int32, (VE - HD, T), 0) == 0, 1.0, 0.0).astype(jnp.bfloat16)

    def blocks(rank):
        keys = jnp.concatenate([kv[rank * 8 + i] for i in range(per)], axis=0)
        vals = jnp.concatenate([kv[rank * 8 + per + i] for i in range(per)], axis=1)
        return keys, jnp.concatenate([vals, ones], axis=0)

    def attend_own():
        keys, vals = blocks(s)
        wide = T // 2
        parts = [(h, half) for h in range(G) for half in range(2)]

        def score(h, half):
            queries = qt[h][:, wide * half : wide * half + wide]
            return jnp.dot(keys[: wide * (half + 1), :], queries, preferred_element_type=jnp.float32)

        ahead = score(*parts[0])
        for i, (h, half) in enumerate(parts):
            scores, count, at = ahead, wide * (half + 1), slice(wide * half, wide * half + wide)
            if i + 1 < len(parts):
                ahead = score(*parts[i + 1])
            key_slot = lax.broadcasted_iota(jnp.int32, (count, wide), 0)
            query_slot = wide * half + lax.broadcasted_iota(jnp.int32, (count, wide), 1)
            allowed = (key_slot >= startr[0:1, at] - s * T) & (key_slot <= query_slot)
            scores = jnp.where(allowed, scores, EXCLUDED)
            top = jnp.max(scores, axis=0, keepdims=True)
            probs = jnp.exp2((scores - top) * SCALE).astype(jnp.bfloat16)
            acc[h, :, at] = jnp.dot(vals[:, :count], probs, preferred_element_type=jnp.float32)
            mx[h, :, at] = top

    def attend(rank):
        keys, vals = blocks(rank)
        key_slot = rank * T + lax.broadcasted_iota(jnp.int32, (T, HD), 0)
        member = (key_slot >= bounds[0:1, :]) & (key_slot < bounds[1:2, :])
        keys = jnp.concatenate([keys, jnp.where(member, 1.0, 0.0).astype(jnp.bfloat16)], axis=1)

        def score(h):
            queries = jnp.concatenate([qt[h], other[...]], axis=0)
            return jnp.dot(keys, queries, preferred_element_type=jnp.float32)

        ahead = score(0)
        for h in range(G):
            scores = ahead
            if h + 1 < G:
                ahead = score(h + 1)
            old = mx[h]
            top = jnp.maximum(old, jnp.max(scores, axis=0, keepdims=True))
            probs = jnp.exp2((scores - top) * SCALE).astype(jnp.bfloat16)
            sums = jnp.dot(vals, probs, preferred_element_type=jnp.float32)
            acc[h] = acc[h] * jnp.exp2((old - top) * SCALE) + sums
            mx[h] = top

    def attend_all(offsets):
        def one(k, carry):
            rank = seq_rank(*offsets[0])
            for i in range(1, len(offsets)):
                rank = jnp.where(k == i, seq_rank(*offsets[i]), rank)

            @pl.when((rank < s) & (rank + 8 >= s))
            def _():
                attend(rank)

            return carry

        lax.fori_loop(0, len(offsets), one, 0)

    attend_own()
    for name, piece in (("xm", 0), ("xp", 1), ("xm", 1), ("xp", 0), ("y", 0), ("y", 1)):
        kv_pass(name, piece)
    for name in ("y", "xm", "xp"):
        kv_share(name)
    gk.wait(seq_rank(0, 0, 1), None, 21)
    attend_all([(0, 0, 1), (0, 1, 0)])
    kv_pass("x2", 0)
    kv_pass("x2", 1)
    kv_share("x2")
    attend_all([(3, 0, 0), (1, 0, 0)])
    for name, piece in (("xmy", 0), ("xpy", 0), ("xmy", 1), ("xpy", 1)):
        kv_pass(name, piece)
    kv_share("xmy")
    kv_share("xpy")
    for name in ("y", "xm", "xp"):
        kv_sib(name)
    attend_all([(0, 1, 1), (3, 0, 1), (1, 0, 1), (3, 1, 0), (1, 1, 0)])
    kv_pass("x2y", 0)
    kv_pass("x2y", 1)
    kv_share("x2y")
    for name in ("x2", "xmy", "xpy"):
        kv_sib(name)
    attend_all([(2, 0, 0), (3, 1, 1), (1, 1, 1), (2, 0, 1), (2, 1, 0)])
    kv_sib("x2y")
    attend_all([(2, 1, 1)])

    for h in range(G):
        o = acc[h, 0:HD, :] * (1.0 / acc[h, HD : HD + 1, :])
        out_ref[:, HD * h : HD * h + HD] = o.T.astype(jnp.bfloat16)

    for i in range(per):
        kc_ref[i, 0] = kv[source[i]]
        page = kv[source[i] + per]
        vc_ref[i, 0] = page.astype(jnp.float32).T.astype(jnp.bfloat16)

    for copy in started:
        copy.wait_send()


def shards(hidden, norm_gain, query_weight, key_weight, value_weight, query_gain, key_gain, lengths, page_table):
    half = 1000000.0 ** -(np.arange(HD // 2, dtype=np.float32) * np.float32(2.0 / HD))
    freq = jnp.asarray(np.concatenate([half, half])[None, :].astype(np.float32))
    vmem = pl.BlockSpec(memory_space=pltpu.VMEM)
    smem = pl.BlockSpec(memory_space=pltpu.SMEM)
    return pl.pallas_call(
        kernel,
        out_shape=(
            jax.ShapeDtypeStruct((T, G * HD), jnp.bfloat16),
            jax.ShapeDtypeStruct((T // PAGE, 1, PAGE, HD), jnp.bfloat16),
            jax.ShapeDtypeStruct((T // PAGE, 1, PAGE, HD), jnp.bfloat16),
        ),
        in_specs=[vmem] * 8 + [smem] * 2,
        out_specs=(vmem,) * 3,
        scratch_shapes=[
            pltpu.VMEM((TP, HR, 256), jnp.bfloat16),
            pltpu.VMEM((D, NC), jnp.bfloat16),
            pltpu.VMEM((SEQ * 8, PAGE, HD), jnp.bfloat16),
            pltpu.VMEM((T, D), jnp.bfloat16),
            pltpu.VMEM((G, HD, T), jnp.bfloat16),
            pltpu.VMEM((G, VE, T), jnp.float32),
            pltpu.VMEM((G, 1, T), jnp.float32),
            pltpu.VMEM((T, HD), jnp.float32),
            pltpu.VMEM((T, HD), jnp.float32),
            pltpu.VMEM((8, T), jnp.int32),
            pltpu.VMEM((HD, T), jnp.bfloat16),
            pltpu.VMEM((8, HD), jnp.int32),
            pltpu.VMEM((T, HD), jnp.float32),
            pltpu.VMEM((TP // 2, T, HD), jnp.bfloat16),
            pltpu.SemaphoreType.DMA((14,)),
            pltpu.SemaphoreType.DMA((14,)),
            pltpu.SemaphoreType.DMA((20,)),
            pltpu.SemaphoreType.DMA((20,)),
            pltpu.SemaphoreType.DMA((22,)),
            pltpu.SemaphoreType.DMA((22,)),
        ],
        compiler_params=pltpu.CompilerParams(
            collective_id=0, has_side_effects=True, vmem_limit_bytes=48 * 1024 * 1024
        ),
        cost_estimate=pl.CostEstimate(flops=7 * 10**9, bytes_accessed=4 * 10**6, transcendentals=10**7),
    )(
        hidden,
        norm_gain,
        query_weight,
        key_weight,
        value_weight,
        query_gain.reshape(1, HD),
        key_gain.reshape(1, HD),
        freq,
        lengths,
        page_table,
    )


def solution(mesh):
    return jax.shard_map(
        shards,
        mesh=mesh,
        in_specs=(
            P("seq", "tp"),
            P(),
            P("seq", "tp"),
            P("seq", "tp"),
            P("seq", "tp"),
            P(),
            P(),
            P(),
            P(),
        ),
        out_specs=(P("seq", "tp"), P("seq", "tp", None, None), P("seq", "tp", None, None)),
        check_vma=False,
    )
```
